1024 devices in a mesh: far: 16 (over z, y_lo), near: 64 (over x, y_hi, core).
Axes of the slice: x: 8, y: 8 (y_hi: 4, y_lo: 2; y = y_hi * 2 + y_lo), z: 8, core: 2. Of those that a mesh axis runs over, the one named last changes fastest.
Arguments:
- state_real: float32 [16, 64, 2, 128, 128], P('far', 'near'), may hold values from -5 to 5
- state_imag: float32 [16, 64, 2, 128, 128], P('far', 'near'), may hold values from -5 to 5
- gate_real: float32 [2, 4, 3, 128, 128], replicated, may hold values from -0.375 to 0.375
- gate_imag: float32 [2, 4, 3, 128, 128], replicated, may hold values from -0.375 to 0.375
Outputs:
- final_real: float32 [16, 64, 2, 128, 128], P('far', 'near')
- final_imag: float32 [16, 64, 2, 128, 128], P('far', 'near')
The draws below stay inside these ranges and needn't reach their ends.
All inputs are finite; a program needn't handle non-finite values.
Results may differ from the reference program's by a relative error of at most 0.000071.
Values sent between devices are 32-bit elements; how exact they have to be, the bound alone decides.
No kernel may reach another device: no remote copies, remote signals or barrier semaphores. Data moves between devices by JAX's collectives and lax.ppermute only.
A program may use at most 32 MiB of HBM per device.

```python
import jax
import jax.numpy as jnp
from jax import lax

GATE = 128
HIGH = 2
ROUNDS = 2
SECTIONS = 4
DEPTH = 3
N_FAR = 16
N_NEAR = 64


def shard_levels(key, shape, cuts, low, high):
    level = 1.0
    for axis_at, parts in cuts:
        heights = jax.random.uniform(jax.random.fold_in(jax.random.fold_in(key, 6), axis_at), (parts,), jnp.float32, low / len(cuts), high / len(cuts))
        level = level * jnp.repeat(jnp.exp(heights), shape[axis_at] // parts).reshape((-1,) + (1,) * (len(shape) - 1 - axis_at))
    return level


def noise(rng, dims, spread, most, cuts=(), kind=jnp.bfloat16):
    array = spread * jax.random.normal(rng, dims, jnp.float32)
    if cuts:
        array = array * shard_levels(rng, dims, cuts, -0.22, 0.18)
    return jnp.clip(array, -most, most).astype(kind)


def setup_inputs(seed: int = 0) -> dict:
    arg_keys = jax.random.split(jax.random.key(seed), 5)
    return {
        "state_real": noise(arg_keys[0], (N_FAR, N_NEAR, HIGH, GATE, GATE), 0.7, 5.0, ((0, 16), (1, 64)), jnp.float32),
        "state_imag": noise(arg_keys[1], (N_FAR, N_NEAR, HIGH, GATE, GATE), 0.7, 5.0, ((0, 16), (1, 64)), jnp.float32),
        "gate_real": noise(arg_keys[2], (ROUNDS, SECTIONS, DEPTH, GATE, GATE), (2 * GATE) ** -0.5, 0.375, (), jnp.float32),
        "gate_imag": noise(arg_keys[3], (ROUNDS, SECTIONS, DEPTH, GATE, GATE), (2 * GATE) ** -0.5, 0.375, (), jnp.float32),
    }


def gate_low(x, g):
    return jnp.einsum('...l,jl->...j', x, g, precision=lax.Precision.HIGHEST, preferred_element_type=jnp.float32)


def gate_mid(x, g):
    return jnp.einsum('...ml,jm->...jl', x, g, precision=lax.Precision.HIGHEST, preferred_element_type=jnp.float32)


def gate_top(x, g):
    high, width, lows = x.shape[-3], x.shape[-2], x.shape[-1]
    upper = g.shape[0] // high
    lead = x.shape[:-3]
    viewed = x.reshape(lead + (high, upper, width // upper, lows))
    matrix = g.reshape((g.shape[0], high, upper))
    out = jnp.einsum('...hkrl,jhk->...jrl', viewed, matrix, precision=lax.Precision.HIGHEST, preferred_element_type=jnp.float32)
    return out.reshape(lead + (high, width, lows))


def complex_gate(form, real, imag, greal, gimag):
    new_real = form(real, greal) - form(imag, gimag)
    new_imag = form(imag, greal) + form(real, gimag)
    return new_real, new_imag


def swap_far(x):
    nfar, nnear, high, width, lows = x.shape
    y = x.reshape((nfar, nnear, nfar, high * width // nfar, lows))
    return jnp.swapaxes(y, 0, 2).reshape(x.shape)


def swap_mid(x):
    nfar, nnear, high, width, lows = x.shape
    y = x.reshape((nfar, nnear, high, nnear, width // nnear, lows))
    return jnp.swapaxes(y, 1, 3).reshape(x.shape)


def swap_low(x):
    nfar, nnear, high, width, lows = x.shape
    y = x.reshape((nfar, nnear, high, width, nnear, lows // nnear))
    return jnp.swapaxes(y, 1, 4).reshape(x.shape)


def swap_top(x):
    nfar, nnear, high, width, lows = x.shape
    y = x.reshape((nfar, nnear, nnear, high * width // nnear, lows))
    return jnp.swapaxes(y, 1, 2).reshape(x.shape)


def reference(state_real, state_imag, gate_real, gate_imag):
    real, imag = state_real, state_imag
    swaps = (swap_far, swap_mid, swap_low, swap_top)
    forms = (gate_low, gate_mid, gate_top)
    for rnd in range(ROUNDS):
        for section in range(4):
            real = swaps[section](real)
            imag = swaps[section](imag)
            for which in range(3):
                real, imag = complex_gate(forms[which], real, imag, gate_real[rnd, section, which], gate_imag[rnd, section, which])
    return real, imag
```

```python
import functools

import jax
import jax.numpy as jnp
from jax import lax
from jax.experimental import pallas as pl
from jax.experimental.pallas import tpu as pltpu
from jax.sharding import PartitionSpec as P

F32, BF16 = jnp.float32, jnp.bfloat16
NN = (((1,), (0,)), ((), ()))
NT = (((1,), (1,)), ((), ()))


def split(x):
    hi = x.astype(BF16)
    return hi, (x - hi.astype(F32)).astype(BF16)


def mm(a, b, dims=NN):
    dot = functools.partial(lax.dot_general, dimension_numbers=dims, preferred_element_type=F32)
    return dot(a[0], b[0]) + (dot(a[0], b[1]) + dot(a[1], b[0]))


def cat(parts, axis):
    return jnp.concatenate(parts, axis)


def rows_of(x, n, count):
    return x[n * count : (n + 1) * count]


def merged(r, n):
    k = r.shape[1] // 2
    return r[:n, :k] - r[n:, k:], r[n:, :k] + r[:n, k:]


def big(real, imag):
    return cat([cat([real, -imag], 1), cat([imag, real], 1)], 0)


def lane_bit(shape, stride):
    return (lax.broadcasted_iota(jnp.int32, shape, 1) // stride) % 2 == 0


def swap(a, b, stride):
    even, lanes = lane_bit(a.shape, stride), a.shape[1]
    return (
        jnp.where(even, a, pltpu.roll(b, stride, 1)),
        jnp.where(even, pltpu.roll(a, lanes - stride, 1), b),
    )


def selector(bit):
    i = lax.broadcasted_iota(jnp.int32, (128, 128), 0)
    j = lax.broadcasted_iota(jnp.int32, (128, 128), 1)
    low, top = i % (1 << bit), i // 64
    mid = (i % 64) // (1 << bit)
    return jnp.where(j == mid * (2 << bit) + top * (1 << bit) + low, 1.0, 0.0).astype(BF16)


def columns_moved(x, sel):
    dot = functools.partial(lax.dot_general, dimension_numbers=NT, preferred_element_type=F32)
    hi, lo = split(x)
    return dot(hi, sel) + dot(lo, sel)


def gate(ref, at):
    return ref[pl.ds(at * 128, 128), :]


def odd_even(ref, at):
    return cat([ref[pl.ds(at * 128 + t, 64, 2), :] for t in range(2)], 0)


def rows_gate(gr, gi, s, sel, top_moved=False):
    mid, top = 3 * s + 1, 3 * s + 2
    m = columns_moved(cat([odd_even(gr, mid), odd_even(gi, mid)], 0), sel)
    if top_moved:
        c = split(cat([odd_even(gr, top), odd_even(gi, top)], 0))
    else:
        c = split(cat([gate(gr, top), gate(gi, top)], 0))
    left = lane_bit((64, 128), 64)
    real, imag = [], []
    for t in range(2):
        row_real, row_imag = [], []
        for u in range(2):
            diagonal = []
            for part in range(2):
                x = rows_of(m, part * 2 + t, 64)
                y = pltpu.roll(x, 64, 1)
                up, down = (x, y) if u == 0 else (y, x)
                diagonal.append(cat([jnp.where(left, up, 0.0), jnp.where(left, 0.0, down)], 0))
            r = mm(c, split(cat(diagonal, 1)))
            wr, wi = merged(r, 128)
            row_real.append(wr)
            row_imag.append(wi)
        real.append(cat(row_real, 1))
        imag.append(cat(row_imag, 1))
    return cat(real, 0), cat(imag, 0)


def product(a, b):
    n = a[0].shape[0]
    r = mm(split(cat(a, 0)), split(cat(b, 1)))
    return merged(r, n)


def low(gr, gi, s):
    return gate(gr, 3 * s), gate(gi, 3 * s)


def put(refs, x):
    refs[0][...], refs[1][...] = split(x)


def prepare_first(gr, gi, w0h, w0l, l25h, l25l):
    sel = selector(0)
    put((w0h, w0l), cat(rows_gate(gr, gi, 0, sel), 0))
    first = tuple(columns_moved(a, sel) for a in low(gr, gi, 2))
    x = product(low(gr, gi, 3), first)
    y = product((odd_even(gr, 15), odd_even(gi, 15)), low(gr, gi, 4))
    put((l25h, l25l), big(*product(y, x)))


def prepare_second(gr, gi, w12h, w12l, w3h, w3l):
    sel = selector(0)
    w = product(rows_gate(gr, gi, 2, sel, True), rows_gate(gr, gi, 1, sel))
    put((w12h, w12l), cat(w, 0))
    put((w3h, w3l), cat(rows_gate(gr, gi, 3, selector(1)), 0))


def prepare_third(gr, gi, w4h, w4l, w56h, w56l, l67h, l67l):
    sel = selector(0)
    put((w4h, w4l), cat(rows_gate(gr, gi, 4, sel), 0))
    w = product(rows_gate(gr, gi, 6, sel, True), rows_gate(gr, gi, 5, sel))
    put((w56h, w56l), cat(w, 0))
    first = tuple(columns_moved(a, sel) for a in low(gr, gi, 6))
    put((l67h, l67l), big(*product(low(gr, gi, 7), first)))


def prepare_fourth(gr, gi, w7h, w7l):
    sel = selector(0)
    w = cat(rows_gate(gr, gi, 7, sel), 0)
    put((w7h, w7l), cat([columns_moved(w[:, :128], sel), columns_moved(w[:, 128:], sel)], 1))


def read_blocks(ref):
    return cat(
        [cat([ref[:, p, t].reshape(128, 128) for t in range(2)], 0) for p in range(2)], 1
    )


def read_strided(ref):
    return cat(
        [cat([ref[pl.ds(p * 4 + o, 64, 8), :] for o in range(4)], 0) for p in range(2)], 1
    )


def phase0(sr, si, g0r, g0i, g1r, g1i, out):
    x = cat([cat([ref[pl.ds(t, 128, 2), :] for t in range(2)], 0) for ref in (sr, si)], 1)
    x = mm(split(x), split(big(g0r[...], g0i[...])), NT)
    x = mm(split(x), split(big(g1r[...], g1i[...])), NT)
    for p in range(2):
        for t in range(2):
            out[:, p, t] = x[t * 128 : (t + 1) * 128, p * 128 : (p + 1) * 128].reshape(16, 8, 128)


def phase1(x, w0h, w0l, l25h, l25l, out):
    o = merged(mm((w0h[...], w0l[...]), split(read_blocks(x))), 256)
    u = [swap(o[p][:128], o[p][128:], 1) for p in range(2)]
    rows = [u[p][v] for p in range(2) for v in range(2)]
    u = cat([cat([rows_of(r, f, 64) for r in rows], 0) for f in range(2)], 1)
    v = mm((l25h[...], l25l[...]), split(u))
    for p in range(2):
        for f in range(2):
            block = v[p * 128 : (p + 1) * 128, f * 128 : (f + 1) * 128]
            for t, y in enumerate(swap(block[:64], block[64:], 1)):
                out[pl.ds(p * 4 + t * 2 + f, 64, 8), :] = y


def phase2(x, w12h, w12l, w3h, w3l, out):
    o = merged(mm((w12h[...], w12l[...]), split(read_strided(x))), 256)
    u = [swap(o[p][:128], o[p][128:], 1) for p in range(2)]
    rows = [u[p][v] for p in range(2) for v in range(2)]
    u = cat([cat([rows_of(r, a, 64) for a in range(2)], 1) for r in rows], 0)
    o = merged(mm((w3h[...], w3l[...]), split(u), NT), 256)
    for p in range(2):
        for t in range(2):
            out[:, p, t] = rows_of(o[p], t, 128).reshape(16, 8, 128)


def phase3(x, w4h, w4l, w56h, w56l, l67h, l67l, out):
    o = merged(mm((w4h[...], w4l[...]), split(read_blocks(x))), 256)
    rows = []
    for p in range(2):
        pairs = [swap(rows_of(o[p], 2 * t, 64), rows_of(o[p], 2 * t + 1, 64), 64) for t in range(2)]
        rows += [cat([pairs[0][v], pairs[1][v]], 1) for v in range(2)]
    o = merged(mm((w56h[...], w56l[...]), split(cat(rows, 0)), NT), 256)
    z = mm(split(cat(o, 1)), (l67h[...], l67l[...]), NT)
    for p in range(2):
        for k in range(4):
            out[pl.ds(p * 4 + k, 64, 8), :] = z[k * 64 : (k + 1) * 64, p * 128 : (p + 1) * 128]


def phase4(x, w7h, w7l, out_real, out_imag):
    o = merged(mm((w7h[...], w7l[...]), split(read_strided(x))), 256)
    for ref, part in zip((out_real, out_imag), o):
        for t in range(2):
            ref[pl.ds(t, 128, 2), :] = rows_of(part, t, 128)


PARAMS = pltpu.CompilerParams(vmem_limit_bytes=48 << 20)
HILO512 = [jax.ShapeDtypeStruct((512, 256), BF16)] * 2
HILO256 = [jax.ShapeDtypeStruct((256, 256), BF16)] * 2


def call(kernel, name, out_shape, flops, *args, in_specs=None):
    more = {} if in_specs is None else {"in_specs": in_specs, "grid": (1,)}
    return pl.pallas_call(
        kernel,
        out_shape=out_shape,
        compiler_params=PARAMS,
        cost_estimate=pl.CostEstimate(flops=flops, bytes_accessed=4 << 20, transcendentals=0),
        name=name,
        **more,
    )(*args)


def on_device(state_real, state_imag, gate_real, gate_imag):
    shape = state_real.shape
    gr, gi = gate_real.reshape(3072, 128), gate_imag.reshape(3072, 128)
    rows = jax.ShapeDtypeStruct((512, 128), F32)
    blocks = jax.ShapeDtypeStruct((16, 2, 2, 8, 128), F32)

    def far(x):
        x = lax.all_to_all(x.reshape(16, 32, 128), "far", 0, 0, tiled=True)
        return x.reshape(16, 2, 2, 8, 128)

    def near(x):
        x = lax.all_to_all(x.reshape(64, 8, 128), "near", 0, 0, tiled=True)
        return x.reshape(512, 128)

    whole = pl.BlockSpec((256, 128), lambda i: (0, 0))
    one = lambda at: pl.BlockSpec((128, 128), lambda i: (at, 0))
    x = call(
        phase0, "phase0", blocks, 200 << 20,
        state_real.reshape(256, 128), state_imag.reshape(256, 128), gr, gi, gr, gi,
        in_specs=[whole, whole, one(0), one(0), one(3), one(3)],
    )
    x = far(x)
    first = call(prepare_first, "prepare_first", HILO512 + HILO256, 400 << 20, gr, gi)
    second = call(prepare_second, "prepare_second", HILO512 + HILO512, 800 << 20, gr, gi)
    third = call(prepare_third, "prepare_third", HILO512 + HILO512 + HILO256, 1200 << 20, gr, gi)
    fourth = call(prepare_fourth, "prepare_fourth", HILO512, 400 << 20, gr, gi)
    x = near(call(phase1, "phase1", rows, 200 << 20, x, *first))
    x = far(call(phase2, "phase2", blocks, 200 << 20, x, *second))
    x = near(call(phase3, "phase3", rows, 200 << 20, x, *third))
    flat = jax.ShapeDtypeStruct((256, 128), F32)
    real, imag = call(phase4, "phase4", [flat, flat], 200 << 20, x, *fourth)
    return real.reshape(shape), imag.reshape(shape)


def solution(mesh):
    spec = P("far", "near", None, None, None)
    return jax.shard_map(
        on_device,
        mesh=mesh,
        in_specs=(spec, spec, P(), P()),
        out_specs=(spec, spec),
        check_vma=False,
    )
```

```python
import functools

import jax
import jax.numpy as jnp
from jax import lax
from jax.experimental import pallas as pl
from jax.experimental.pallas import tpu as pltpu
from jax.sharding import PartitionSpec as P

F32, BF16 = jnp.float32, jnp.bfloat16
NN = (((1,), (0,)), ((), ()))
NT = (((1,), (1,)), ((), ()))


def split(x):
    hi = x.astype(BF16)
    return hi, (x - hi.astype(F32)).astype(BF16)


def mm(a, b, dims=NN):
    dot = functools.partial(lax.dot_general, dimension_numbers=dims, preferred_element_type=F32)
    return dot(a[0], b[0]) + (dot(a[0], b[1]) + dot(a[1], b[0]))


def cat(parts, axis):
    return jnp.concatenate(parts, axis)


def rows_of(x, n, count):
    return x[n * count : (n + 1) * count]


def merged(r, n):
    k = r.shape[1] // 2
    return r[:n, :k] - r[n:, k:], r[n:, :k] + r[:n, k:]


def big(real, imag):
    return cat([cat([real, -imag], 1), cat([imag, real], 1)], 0)


def lane_bit(shape, stride):
    return (lax.broadcasted_iota(jnp.int32, shape, 1) // stride) % 2 == 0


def swap(a, b, stride):
    even, lanes = lane_bit(a.shape, stride), a.shape[1]
    return (
        jnp.where(even, a, pltpu.roll(b, stride, 1)),
        jnp.where(even, pltpu.roll(a, lanes - stride, 1), b),
    )


def selector(bit):
    i = lax.broadcasted_iota(jnp.int32, (128, 128), 0)
    j = lax.broadcasted_iota(jnp.int32, (128, 128), 1)
    low, top = i % (1 << bit), i // 64
    mid = (i % 64) // (1 << bit)
    return jnp.where(j == mid * (2 << bit) + top * (1 << bit) + low, 1.0, 0.0).astype(BF16)


def columns_moved(x, sel):
    dot = functools.partial(lax.dot_general, dimension_numbers=NT, preferred_element_type=F32)
    hi, lo = split(x)
    return dot(hi, sel) + dot(lo, sel)


def gate(ref, at):
    return ref[pl.ds(at * 128, 128), :]


def odd_even(ref, at):
    return cat([ref[pl.ds(at * 128 + t, 64, 2), :] for t in range(2)], 0)


def rows_gate(gr, gi, s, sel, top_moved=False):
    mid, top = 3 * s + 1, 3 * s + 2
    m = columns_moved(cat([odd_even(gr, mid), odd_even(gi, mid)], 0), sel)
    if top_moved:
        c = split(cat([odd_even(gr, top), odd_even(gi, top)], 0))
    else:
        c = split(cat([gate(gr, top), gate(gi, top)], 0))
    left = lane_bit((64, 128), 64)
    real, imag = [], []
    for t in range(2):
        row_real, row_imag = [], []
        for u in range(2):
            diagonal = []
            for part in range(2):
                x = rows_of(m, part * 2 + t, 64)
                y = pltpu.roll(x, 64, 1)
                up, down = (x, y) if u == 0 else (y, x)
                diagonal.append(cat([jnp.where(left, up, 0.0), jnp.where(left, 0.0, down)], 0))
            r = mm(c, split(cat(diagonal, 1)))
            wr, wi = merged(r, 128)
            row_real.append(wr)
            row_imag.append(wi)
        real.append(cat(row_real, 1))
        imag.append(cat(row_imag, 1))
    return cat(real, 0), cat(imag, 0)


def product(a, b):
    n = a[0].shape[0]
    r = mm(split(cat(a, 0)), split(cat(b, 1)))
    return merged(r, n)


def low(gr, gi, s):
    return gate(gr, 3 * s), gate(gi, 3 * s)


def fetched(first, last):
    def wrap(kernel):
        def run(gr, gi, *rest):
            outs, (vr, vi, sems) = rest[:-3], rest[-3:]
            rows = pl.ds(first * 128, (last - first) * 128)
            copies = [
                pltpu.make_async_copy(src.at[rows], dst.at[rows], sems.at[k])
                for k, (src, dst) in enumerate(((gr, vr), (gi, vi)))
            ]
            for copy in copies:
                copy.start()
            for copy in copies:
                copy.wait()
            kernel(vr, vi, *outs)

        return run

    return wrap


def put(refs, x):
    refs[0][...], refs[1][...] = split(x)


@fetched(0, 16)
def prepare_first(gr, gi, w0h, w0l, l25h, l25l):
    sel = selector(0)
    put((w0h, w0l), cat(rows_gate(gr, gi, 0, sel), 0))
    first = tuple(columns_moved(a, sel) for a in low(gr, gi, 2))
    x = product(low(gr, gi, 3), first)
    y = product((odd_even(gr, 15), odd_even(gi, 15)), low(gr, gi, 4))
    put((l25h, l25l), big(*product(y, x)))


@fetched(3, 12)
def prepare_second(gr, gi, w12h, w12l, w3h, w3l):
    sel = selector(0)
    w = product(rows_gate(gr, gi, 2, sel, True), rows_gate(gr, gi, 1, sel))
    put((w12h, w12l), cat(w, 0))
    put((w3h, w3l), cat(rows_gate(gr, gi, 3, selector(1)), 0))


@fetched(12, 24)
def prepare_third(gr, gi, w4h, w4l, w56h, w56l, l67h, l67l):
    sel = selector(0)
    put((w4h, w4l), cat(rows_gate(gr, gi, 4, sel), 0))
    w = product(rows_gate(gr, gi, 6, sel, True), rows_gate(gr, gi, 5, sel))
    put((w56h, w56l), cat(w, 0))
    first = tuple(columns_moved(a, sel) for a in low(gr, gi, 6))
    put((l67h, l67l), big(*product(low(gr, gi, 7), first)))


@fetched(21, 24)
def prepare_fourth(gr, gi, w7h, w7l):
    sel = selector(0)
    w = cat(rows_gate(gr, gi, 7, sel), 0)
    put((w7h, w7l), cat([columns_moved(w[:, :128], sel), columns_moved(w[:, 128:], sel)], 1))


def read_blocks(ref):
    return cat(
        [cat([ref[:, p, t].reshape(128, 128) for t in range(2)], 0) for p in range(2)], 1
    )


def read_strided(ref):
    return cat(
        [cat([ref[pl.ds(p * 4 + o, 64, 8), :] for o in range(4)], 0) for p in range(2)], 1
    )


def phase0(sr, si, gr, gi, out, vr, vi, g0r, g0i, g1r, g1i, sems):
    zero, one = pl.ds(0, 128), pl.ds(3 * 128, 128)
    pairs = [
        (sr, vr), (si, vi), (gr.at[zero], g0r), (gi.at[zero], g0i), (gr.at[one], g1r), (gi.at[one], g1i),
    ]
    copies = [pltpu.make_async_copy(a, b, sems.at[k]) for k, (a, b) in enumerate(pairs)]
    for copy in copies:
        copy.start()
    for copy in copies:
        copy.wait()
    x = cat([cat([ref[pl.ds(t, 128, 2), :] for t in range(2)], 0) for ref in (vr, vi)], 1)
    x = mm(split(x), split(big(g0r[...], g0i[...])), NT)
    x = mm(split(x), split(big(g1r[...], g1i[...])), NT)
    for p in range(2):
        for t in range(2):
            out[:, p, t] = x[t * 128 : (t + 1) * 128, p * 128 : (p + 1) * 128].reshape(16, 8, 128)


def phase1(x, w0h, w0l, l25h, l25l, out):
    o = merged(mm((w0h[...], w0l[...]), split(read_blocks(x))), 256)
    u = [swap(o[p][:128], o[p][128:], 1) for p in range(2)]
    rows = [u[p][v] for p in range(2) for v in range(2)]
    u = cat([cat([rows_of(r, f, 64) for r in rows], 0) for f in range(2)], 1)
    v = mm((l25h[...], l25l[...]), split(u))
    for p in range(2):
        for f in range(2):
            block = v[p * 128 : (p + 1) * 128, f * 128 : (f + 1) * 128]
            for t, y in enumerate(swap(block[:64], block[64:], 1)):
                out[pl.ds(p * 4 + t * 2 + f, 64, 8), :] = y


def phase2(x, w12h, w12l, w3h, w3l, out):
    o = merged(mm((w12h[...], w12l[...]), split(read_strided(x))), 256)
    u = [swap(o[p][:128], o[p][128:], 1) for p in range(2)]
    rows = [u[p][v] for p in range(2) for v in range(2)]
    u = cat([cat([rows_of(r, a, 64) for a in range(2)], 1) for r in rows], 0)
    o = merged(mm((w3h[...], w3l[...]), split(u), NT), 256)
    for p in range(2):
        for t in range(2):
            out[:, p, t] = rows_of(o[p], t, 128).reshape(16, 8, 128)


def phase3(x, w4h, w4l, w56h, w56l, l67h, l67l, out):
    o = merged(mm((w4h[...], w4l[...]), split(read_blocks(x))), 256)
    rows = []
    for p in range(2):
        pairs = [swap(rows_of(o[p], 2 * t, 64), rows_of(o[p], 2 * t + 1, 64), 64) for t in range(2)]
        rows += [cat([pairs[0][v], pairs[1][v]], 1) for v in range(2)]
    o = merged(mm((w56h[...], w56l[...]), split(cat(rows, 0)), NT), 256)
    z = mm(split(cat(o, 1)), (l67h[...], l67l[...]), NT)
    for p in range(2):
        for k in range(4):
            out[pl.ds(p * 4 + k, 64, 8), :] = z[k * 64 : (k + 1) * 64, p * 128 : (p + 1) * 128]


def phase4(x, w7h, w7l, out_real, out_imag):
    o = merged(mm((w7h[...], w7l[...]), split(read_strided(x))), 256)
    for ref, part in zip((out_real, out_imag), o):
        for t in range(2):
            ref[pl.ds(t, 128, 2), :] = rows_of(part, t, 128)


PARAMS = pltpu.CompilerParams(vmem_limit_bytes=48 << 20)
HILO512 = [jax.ShapeDtypeStruct((512, 256), BF16)] * 2
HILO256 = [jax.ShapeDtypeStruct((256, 256), BF16)] * 2


def call(kernel, name, out_shape, flops, *args, scratch=None):
    more = {}
    if scratch is not None:
        in_hbm = pl.BlockSpec(memory_space=pltpu.HBM)
        more = {"in_specs": [in_hbm] * len(args), "scratch_shapes": scratch}
    return pl.pallas_call(
        kernel,
        out_shape=out_shape,
        compiler_params=PARAMS,
        cost_estimate=pl.CostEstimate(flops=flops, bytes_accessed=4 << 20, transcendentals=0),
        name=name,
        **more,
    )(*args)


def on_device(state_real, state_imag, gate_real, gate_imag):
    shape = state_real.shape
    gr, gi = gate_real.reshape(3072, 128), gate_imag.reshape(3072, 128)
    gr, gi, sr, si = (
        pltpu.with_memory_space_constraint(a, pltpu.HBM)
        for a in (gr, gi, state_real.reshape(256, 128), state_imag.reshape(256, 128))
    )
    rows = jax.ShapeDtypeStruct((512, 128), F32)
    blocks = jax.ShapeDtypeStruct((16, 2, 2, 8, 128), F32)

    def far(x):
        x = lax.all_to_all(x.reshape(16, 32, 128), "far", 0, 0, tiled=True)
        return x.reshape(16, 2, 2, 8, 128)

    def near(x):
        x = lax.all_to_all(x.reshape(64, 8, 128), "near", 0, 0, tiled=True)
        return x.reshape(512, 128)

    state = pltpu.VMEM((256, 128), F32)
    matrix = pltpu.VMEM((128, 128), F32)
    x = call(
        phase0, "phase0", blocks, 200 << 20,
        sr, si, gr, gi,
        scratch=[state, state] + [matrix] * 4 + [pltpu.SemaphoreType.DMA((6,))],
    )
    gates = [pltpu.VMEM((3072, 128), F32)] * 2 + [pltpu.SemaphoreType.DMA((2,))]
    x = far(x)
    first = call(prepare_first, "prepare_first", HILO512 + HILO256, 400 << 20, gr, gi, scratch=gates)
    second = call(prepare_second, "prepare_second", HILO512 + HILO512, 800 << 20, gr, gi, scratch=gates)
    third = call(prepare_third, "prepare_third", HILO512 + HILO512 + HILO256, 1200 << 20, gr, gi, scratch=gates)
    fourth = call(prepare_fourth, "prepare_fourth", HILO512, 400 << 20, gr, gi, scratch=gates)
    x = near(call(phase1, "phase1", rows, 200 << 20, x, *first))
    x = far(call(phase2, "phase2", blocks, 200 << 20, x, *second))
    x = near(call(phase3, "phase3", rows, 200 << 20, x, *third))
    flat = jax.ShapeDtypeStruct((256, 128), F32)
    real, imag = call(phase4, "phase4", [flat, flat], 200 << 20, x, *fourth)
    return real.reshape(shape), imag.reshape(shape)


def solution(mesh):
    spec = P("far", "near", None, None, None)
    return jax.shard_map(
        on_device,
        mesh=mesh,
        in_specs=(spec, spec, P(), P()),
        out_specs=(spec, spec),
        check_vma=False,
    )
```

```python
import functools

import jax
import jax.numpy as jnp
from jax import lax
from jax.experimental import pallas as pl
from jax.experimental.pallas import tpu as pltpu
from jax.sharding import PartitionSpec as P

F32, BF16 = jnp.float32, jnp.bfloat16
NN = (((1,), (0,)), ((), ()))
NT = (((1,), (1,)), ((), ()))


def split(x):
    hi = x.astype(BF16)
    return hi, (x - hi.astype(F32)).astype(BF16)


def mm(a, b, dims=NN):
    dot = functools.partial(lax.dot_general, dimension_numbers=dims, preferred_element_type=F32)
    return dot(a[0], b[0]) + (dot(a[0], b[1]) + dot(a[1], b[0]))


def cat(parts, axis):
    return jnp.concatenate(parts, axis)


def rows_of(x, n, count):
    return x[n * count : (n + 1) * count]


def merged(r, n):
    k = r.shape[1] // 2
    return r[:n, :k] - r[n:, k:], r[n:, :k] + r[:n, k:]


def big(real, imag):
    return cat([cat([real, -imag], 1), cat([imag, real], 1)], 0)


def lane_bit(shape, stride):
    return (lax.broadcasted_iota(jnp.int32, shape, 1) // stride) % 2 == 0


def swap(a, b, stride):
    even, lanes = lane_bit(a.shape, stride), a.shape[1]
    return (
        jnp.where(even, a, pltpu.roll(b, stride, 1)),
        jnp.where(even, pltpu.roll(a, lanes - stride, 1), b),
    )


def selector(bit):
    i = lax.broadcasted_iota(jnp.int32, (128, 128), 0)
    j = lax.broadcasted_iota(jnp.int32, (128, 128), 1)
    low, top = i % (1 << bit), i // 64
    mid = (i % 64) // (1 << bit)
    return jnp.where(j == mid * (2 << bit) + top * (1 << bit) + low, 1.0, 0.0).astype(BF16)


def columns_moved(x, sel):
    dot = functools.partial(lax.dot_general, dimension_numbers=NT, preferred_element_type=F32)
    hi, lo = split(x)
    return dot(hi, sel) + dot(lo, sel)


def gate(ref, at):
    return ref[pl.ds(at * 128, 128), :]


def odd_even(ref, at):
    return cat([ref[pl.ds(at * 128 + t, 64, 2), :] for t in range(2)], 0)


def rows_gate_plain(gr, gi, s):
    m = [odd_even(ref, 3 * s + 1) for ref in (gr, gi)]
    c = split(cat([gate(ref, 3 * s + 2) for ref in (gr, gi)], 0))
    zero = jnp.zeros((64, 128), F32)
    real, imag = [], []
    for t in range(2):
        diagonal = []
        for part in range(2):
            x = rows_of(m[part], t, 64)
            diagonal.append(cat([cat([x, zero], 1), cat([zero, x], 1)], 0))
        wr, wi = merged(mm(c, split(cat(diagonal, 1))), 128)
        real.append(wr)
        imag.append(wi)
    return cat(real, 0), cat(imag, 0)


def rows_gate(gr, gi, s, sel, top_moved=False):
    mid, top = 3 * s + 1, 3 * s + 2
    m = columns_moved(cat([odd_even(gr, mid), odd_even(gi, mid)], 0), sel)
    if top_moved:
        c = split(cat([odd_even(gr, top), odd_even(gi, top)], 0))
    else:
        c = split(cat([gate(gr, top), gate(gi, top)], 0))
    left = lane_bit((64, 128), 64)
    real, imag = [], []
    for t in range(2):
        row_real, row_imag = [], []
        for u in range(2):
            diagonal = []
            for part in range(2):
                x = rows_of(m, part * 2 + t, 64)
                y = pltpu.roll(x, 64, 1)
                up, down = (x, y) if u == 0 else (y, x)
                diagonal.append(cat([jnp.where(left, up, 0.0), jnp.where(left, 0.0, down)], 0))
            r = mm(c, split(cat(diagonal, 1)))
            wr, wi = merged(r, 128)
            row_real.append(wr)
            row_imag.append(wi)
        real.append(cat(row_real, 1))
        imag.append(cat(row_imag, 1))
    return cat(real, 0), cat(imag, 0)


def product(a, b):
    n = a[0].shape[0]
    r = mm(split(cat(a, 0)), split(cat(b, 1)))
    return merged(r, n)


def low(gr, gi, s):
    return gate(gr, 3 * s), gate(gi, 3 * s)


def fetched(first, last):
    def wrap(kernel):
        def run(gr, gi, *rest):
            outs, (vr, vi, sems) = rest[:-3], rest[-3:]
            rows = pl.ds(first * 128, (last - first) * 128)
            copies = [
                pltpu.make_async_copy(src.at[rows], dst.at[rows], sems.at[k])
                for k, (src, dst) in enumerate(((gr, vr), (gi, vi)))
            ]
            for copy in copies:
                copy.start()
            for copy in copies:
                copy.wait()
            kernel(vr, vi, *outs)

        return run

    return wrap


def put(refs, x):
    refs[0][...], refs[1][...] = split(x)


@fetched(0, 16)
def prepare_first(gr, gi, l01h, l01l, w0h, w0l, l25h, l25l, w12h, w12l, w3h, w3l):
    sel = selector(0)
    put((l01h, l01l), big(*product(low(gr, gi, 1), low(gr, gi, 0))))
    put((w0h, w0l), cat(rows_gate_plain(gr, gi, 0), 0))
    first = tuple(columns_moved(a, sel) for a in low(gr, gi, 2))
    x = product(low(gr, gi, 3), first)
    y = product((odd_even(gr, 15), odd_even(gi, 15)), low(gr, gi, 4))
    put((l25h, l25l), big(*product(y, x)))
    w = product(rows_gate(gr, gi, 2, sel, True), rows_gate(gr, gi, 1, sel))
    put((w12h, w12l), cat(w, 0))
    put((w3h, w3l), cat(rows_gate(gr, gi, 3, selector(1)), 0))


@fetched(12, 24)
def prepare_second(gr, gi, w4h, w4l, w56h, w56l, l67h, l67l, w7h, w7l):
    sel = selector(0)
    put((w4h, w4l), cat(rows_gate(gr, gi, 4, sel), 0))
    w = product(rows_gate(gr, gi, 6, sel, True), rows_gate(gr, gi, 5, sel))
    put((w56h, w56l), cat(w, 0))
    first = tuple(columns_moved(a, sel) for a in low(gr, gi, 6))
    put((l67h, l67l), big(*product(low(gr, gi, 7), first)))
    w = cat(rows_gate(gr, gi, 7, sel), 0)
    put((w7h, w7l), cat([columns_moved(w[:, :128], sel), columns_moved(w[:, 128:], sel)], 1))


def read_blocks(ref):
    return cat(
        [cat([ref[:, p, t].reshape(128, 128) for t in range(2)], 0) for p in range(2)], 1
    )


def read_strided(ref):
    return cat(
        [cat([ref[pl.ds(p * 4 + o, 64, 8), :] for o in range(4)], 0) for p in range(2)], 1
    )


def phase0(sr, si, out, sems):
    copies = [
        pltpu.make_async_copy(ref, out.at[:, p], sems.at[p]) for p, ref in enumerate((sr, si))
    ]
    for copy in copies:
        copy.start()
    for copy in copies:
        copy.wait()


def phase1(x, l01h, l01l, w0h, w0l, l25h, l25l, out):
    y = cat([x[:, p].reshape(256, 128) for p in range(2)], 1)
    y = mm(split(y), (l01h[...], l01l[...]), NT)
    o = merged(mm((w0h[...], w0l[...]), split(y)), 256)
    u = [swap(o[p][:128], o[p][128:], 1) for p in range(2)]
    rows = [u[p][v] for p in range(2) for v in range(2)]
    u = cat([cat([rows_of(r, f, 64) for r in rows], 0) for f in range(2)], 1)
    v = mm((l25h[...], l25l[...]), split(u))
    for p in range(2):
        for f in range(2):
            block = v[p * 128 : (p + 1) * 128, f * 128 : (f + 1) * 128]
            for t, y in enumerate(swap(block[:64], block[64:], 1)):
                out[pl.ds(p * 4 + t * 2 + f, 64, 8), :] = y


def phase2(x, w12h, w12l, w3h, w3l, out):
    o = merged(mm((w12h[...], w12l[...]), split(read_strided(x))), 256)
    u = [swap(o[p][:128], o[p][128:], 1) for p in range(2)]
    rows = [u[p][v] for p in range(2) for v in range(2)]
    u = cat([cat([rows_of(r, a, 64) for a in range(2)], 1) for r in rows], 0)
    o = merged(mm((w3h[...], w3l[...]), split(u), NT), 256)
    for p in range(2):
        for t in range(2):
            out[:, p, t] = rows_of(o[p], t, 128).reshape(16, 8, 128)


def phase3(x, w4h, w4l, w56h, w56l, l67h, l67l, out):
    o = merged(mm((w4h[...], w4l[...]), split(read_blocks(x))), 256)
    rows = []
    for p in range(2):
        pairs = [swap(rows_of(o[p], 2 * t, 64), rows_of(o[p], 2 * t + 1, 64), 64) for t in range(2)]
        rows += [cat([pairs[0][v], pairs[1][v]], 1) for v in range(2)]
    o = merged(mm((w56h[...], w56l[...]), split(cat(rows, 0)), NT), 256)
    z = mm(split(cat(o, 1)), (l67h[...], l67l[...]), NT)
    for p in range(2):
        for k in range(4):
            out[pl.ds(p * 4 + k, 64, 8), :] = z[k * 64 : (k + 1) * 64, p * 128 : (p + 1) * 128]


def phase4(x, w7h, w7l, out_real, out_imag):
    o = merged(mm((w7h[...], w7l[...]), split(read_strided(x))), 256)
    for ref, part in zip((out_real, out_imag), o):
        for t in range(2):
            ref[pl.ds(t, 128, 2), :] = rows_of(part, t, 128)


PARAMS = pltpu.CompilerParams(vmem_limit_bytes=48 << 20)
HILO512 = [jax.ShapeDtypeStruct((512, 256), BF16)] * 2
HILO256 = [jax.ShapeDtypeStruct((256, 256), BF16)] * 2


def call(kernel, name, out_shape, flops, *args, scratch=None, out_specs=None):
    more = {}
    if scratch is not None:
        in_hbm = pl.BlockSpec(memory_space=pltpu.HBM)
        more = {"in_specs": [in_hbm] * len(args), "scratch_shapes": scratch}
    if out_specs is not None:
        more["out_specs"] = out_specs
    return pl.pallas_call(
        kernel,
        out_shape=out_shape,
        compiler_params=PARAMS,
        cost_estimate=pl.CostEstimate(flops=flops, bytes_accessed=4 << 20, transcendentals=0),
        name=name,
        **more,
    )(*args)


def on_device(state_real, state_imag, gate_real, gate_imag):
    shape = state_real.shape
    sr, si, gr, gi = (
        pltpu.with_memory_space_constraint(a, pltpu.HBM)
        for a in (
            state_real.reshape(16, 16, 128), state_imag.reshape(16, 16, 128),
            gate_real.reshape(3072, 128), gate_imag.reshape(3072, 128),
        )
    )
    rows = jax.ShapeDtypeStruct((512, 128), F32)
    blocks = jax.ShapeDtypeStruct((16, 2, 2, 8, 128), F32)

    def far(x):
        return lax.all_to_all(x.reshape(16, 32, 128), "far", 0, 0, tiled=True)

    def near(x):
        x = lax.all_to_all(x.reshape(64, 8, 128), "near", 0, 0, tiled=True)
        return x.reshape(512, 128)

    x = call(
        phase0, "phase0", jax.ShapeDtypeStruct((16, 2, 16, 128), F32), 1 << 20, sr, si,
        scratch=[pltpu.SemaphoreType.DMA((2,))], out_specs=pl.BlockSpec(memory_space=pltpu.HBM),
    )
    gates = [pltpu.VMEM((3072, 128), F32)] * 2 + [pltpu.SemaphoreType.DMA((2,))]
    x = far(x)
    first = call(
        prepare_first, "prepare_first", HILO256 + HILO512 + HILO256 + HILO512 + HILO512, 1200 << 20,
        gr, gi, scratch=gates,
    )
    x = near(call(phase1, "phase1", rows, 200 << 20, x.reshape(16, 2, 16, 128), *first[:6]))
    x = far(call(phase2, "phase2", blocks, 200 << 20, x, *first[6:]))
    second = call(
        prepare_second, "prepare_second", HILO512 + HILO512 + HILO256 + HILO512, 1600 << 20,
        gr, gi, scratch=gates,
    )
    x = x.reshape(16, 2, 2, 8, 128)
    x = near(call(phase3, "phase3", rows, 200 << 20, x, *second[:6]))
    flat = jax.ShapeDtypeStruct((256, 128), F32)
    real, imag = call(phase4, "phase4", [flat, flat], 200 << 20, x, *second[6:])
    return real.reshape(shape), imag.reshape(shape)


def solution(mesh):
    spec = P("far", "near", None, None, None)
    return jax.shard_map(
        on_device,
        mesh=mesh,
        in_specs=(spec, spec, P(), P()),
        out_specs=(spec, spec),
        check_vma=False,
    )
```

```python
import functools

import jax
import jax.numpy as jnp
from jax import lax
from jax.experimental import pallas as pl
from jax.experimental.pallas import tpu as pltpu
from jax.sharding import PartitionSpec as P

F32, BF16 = jnp.float32, jnp.bfloat16
NN = (((1,), (0,)), ((), ()))
NT = (((1,), (1,)), ((), ()))


def split(x):
    hi = x.astype(BF16)
    return hi, (x - hi.astype(F32)).astype(BF16)


def mm(a, b, dims=NN):
    dot = functools.partial(lax.dot_general, dimension_numbers=dims, preferred_element_type=F32)
    return dot(a[0], b[0]) + (dot(a[0], b[1]) + dot(a[1], b[0]))


def cat(parts, axis):
    return jnp.concatenate(parts, axis)


def rows_of(x, n, count):
    return x[n * count : (n + 1) * count]


def merged(r, n):
    k = r.shape[1] // 2
    return r[:n, :k] - r[n:, k:], r[n:, :k] + r[:n, k:]


def big(real, imag):
    return cat([cat([real, -imag], 1), cat([imag, real], 1)], 0)


def lane_bit(shape, stride):
    return (lax.broadcasted_iota(jnp.int32, shape, 1) // stride) % 2 == 0


def swap(a, b, stride):
    even, lanes = lane_bit(a.shape, stride), a.shape[1]
    return (
        jnp.where(even, a, pltpu.roll(b, stride, 1)),
        jnp.where(even, pltpu.roll(a, lanes - stride, 1), b),
    )


def selector(bit):
    i = lax.broadcasted_iota(jnp.int32, (128, 128), 0)
    j = lax.broadcasted_iota(jnp.int32, (128, 128), 1)
    low, top = i % (1 << bit), i // 64
    mid = (i % 64) // (1 << bit)
    return jnp.where(j == mid * (2 << bit) + top * (1 << bit) + low, 1.0, 0.0).astype(BF16)


def columns_moved(x, sel):
    dot = functools.partial(lax.dot_general, dimension_numbers=NT, preferred_element_type=F32)
    hi, lo = split(x)
    return dot(hi, sel) + dot(lo, sel)


def gate(ref, at):
    return ref[pl.ds(at * 128, 128), :]


def odd_even(ref, at):
    return cat([ref[pl.ds(at * 128 + t, 64, 2), :] for t in range(2)], 0)


def rows_gate_plain(gr, gi, s):
    m = [odd_even(ref, 3 * s + 1) for ref in (gr, gi)]
    c = split(cat([gate(ref, 3 * s + 2) for ref in (gr, gi)], 0))
    zero = jnp.zeros((64, 128), F32)
    real, imag = [], []
    for t in range(2):
        diagonal = []
        for part in range(2):
            x = rows_of(m[part], t, 64)
            diagonal.append(cat([cat([x, zero], 1), cat([zero, x], 1)], 0))
        wr, wi = merged(mm(c, split(cat(diagonal, 1))), 128)
        real.append(wr)
        imag.append(wi)
    return cat(real, 0), cat(imag, 0)


def rows_gate(gr, gi, s, sel, top_moved=False):
    mid, top = 3 * s + 1, 3 * s + 2
    m = columns_moved(cat([odd_even(gr, mid), odd_even(gi, mid)], 0), sel)
    if top_moved:
        c = split(cat([odd_even(gr, top), odd_even(gi, top)], 0))
    else:
        c = split(cat([gate(gr, top), gate(gi, top)], 0))
    left = lane_bit((64, 128), 64)
    real, imag = [], []
    for t in range(2):
        row_real, row_imag = [], []
        for u in range(2):
            diagonal = []
            for part in range(2):
                x = rows_of(m, part * 2 + t, 64)
                y = pltpu.roll(x, 64, 1)
                up, down = (x, y) if u == 0 else (y, x)
                diagonal.append(cat([jnp.where(left, up, 0.0), jnp.where(left, 0.0, down)], 0))
            r = mm(c, split(cat(diagonal, 1)))
            wr, wi = merged(r, 128)
            row_real.append(wr)
            row_imag.append(wi)
        real.append(cat(row_real, 1))
        imag.append(cat(row_imag, 1))
    return cat(real, 0), cat(imag, 0)


def product(a, b):
    n = a[0].shape[0]
    r = mm(split(cat(a, 0)), split(cat(b, 1)))
    return merged(r, n)


def low(gr, gi, s):
    return gate(gr, 3 * s), gate(gi, 3 * s)


def fetched(first, last):
    def wrap(kernel):
        def run(gr, gi, *rest):
            outs, (vr, vi, sems) = rest[:-3], rest[-3:]
            rows = pl.ds(first * 128, (last - first) * 128)
            copies = [
                pltpu.make_async_copy(src.at[rows], dst.at[rows], sems.at[k])
                for k, (src, dst) in enumerate(((gr, vr), (gi, vi)))
            ]
            for copy in copies:
                copy.start()
            for copy in copies:
                copy.wait()
            kernel(vr, vi, *outs)

        return run

    return wrap


def put(refs, x):
    refs[0][...], refs[1][...] = split(x)


@fetched(0, 16)
def prepare_first(gr, gi, l01h, l01l, w0h, w0l, l25h, l25l, w12h, w12l, w3h, w3l):
    sel = selector(0)
    put((l01h, l01l), big(*product(low(gr, gi, 1), low(gr, gi, 0))))
    put((w0h, w0l), cat(rows_gate_plain(gr, gi, 0), 0))
    first = tuple(columns_moved(a, sel) for a in low(gr, gi, 2))
    x = product(low(gr, gi, 3), first)
    y = product((odd_even(gr, 15), odd_even(gi, 15)), low(gr, gi, 4))
    put((l25h, l25l), big(*product(y, x)))
    w = product(rows_gate(gr, gi, 2, sel, True), rows_gate(gr, gi, 1, sel))
    put((w12h, w12l), cat(w, 0))
    put((w3h, w3l), cat(rows_gate(gr, gi, 3, selector(1)), 0))


@fetched(12, 24)
def prepare_second(gr, gi, w4h, w4l, w56h, w56l, l67h, l67l, w7h, w7l):
    sel = selector(0)
    put((w4h, w4l), cat(rows_gate(gr, gi, 4, sel), 0))
    w = product(rows_gate(gr, gi, 6, sel, True), rows_gate(gr, gi, 5, sel))
    put((w56h, w56l), cat(w, 0))
    first = tuple(columns_moved(a, sel) for a in low(gr, gi, 6))
    put((l67h, l67l), big(*product(low(gr, gi, 7), first)))
    w = cat(rows_gate(gr, gi, 7, sel), 0)
    put((w7h, w7l), cat([columns_moved(w[:, :128], sel), columns_moved(w[:, 128:], sel)], 1))


def read_blocks(ref):
    return cat(
        [cat([ref[:, p, t].reshape(128, 128) for t in range(2)], 0) for p in range(2)], 1
    )


def read_strided(ref):
    return cat(
        [cat([ref[pl.ds(p * 4 + o, 64, 8), :] for o in range(4)], 0) for p in range(2)], 1
    )


def phase0(sr, si, out, vr, vi, sems):
    pairs = [(sr, vr), (si, vi)]
    copies = [pltpu.make_async_copy(a, b, sems.at[p]) for p, (a, b) in enumerate(pairs)]
    for copy in copies:
        copy.start()
    for p, copy in enumerate(copies):
        copy.wait()
        out[:, p] = pairs[p][1][...]


def phase1(x, l01h, l01l, w0h, w0l, l25h, l25l, out):
    y = cat([x[:, p].reshape(256, 128) for p in range(2)], 1)
    y = mm(split(y), (l01h[...], l01l[...]), NT)
    o = merged(mm((w0h[...], w0l[...]), split(y)), 256)
    u = [swap(o[p][:128], o[p][128:], 1) for p in range(2)]
    rows = [u[p][v] for p in range(2) for v in range(2)]
    u = cat([cat([rows_of(r, f, 64) for r in rows], 0) for f in range(2)], 1)
    v = mm((l25h[...], l25l[...]), split(u))
    for p in range(2):
        for f in range(2):
            block = v[p * 128 : (p + 1) * 128, f * 128 : (f + 1) * 128]
            for t, y in enumerate(swap(block[:64], block[64:], 1)):
                out[pl.ds(p * 4 + t * 2 + f, 64, 8), :] = y


def phase2(x, w12h, w12l, w3h, w3l, out):
    o = merged(mm((w12h[...], w12l[...]), split(read_strided(x))), 256)
    u = [swap(o[p][:128], o[p][128:], 1) for p in range(2)]
    rows = [u[p][v] for p in range(2) for v in range(2)]
    u = cat([cat([rows_of(r, a, 64) for a in range(2)], 1) for r in rows], 0)
    o = merged(mm((w3h[...], w3l[...]), split(u), NT), 256)
    for p in range(2):
        for t in range(2):
            out[:, p, t] = rows_of(o[p], t, 128).reshape(16, 8, 128)


def phase3(x, w4h, w4l, w56h, w56l, l67h, l67l, out):
    o = merged(mm((w4h[...], w4l[...]), split(read_blocks(x))), 256)
    rows = []
    for p in range(2):
        pairs = [swap(rows_of(o[p], 2 * t, 64), rows_of(o[p], 2 * t + 1, 64), 64) for t in range(2)]
        rows += [cat([pairs[0][v], pairs[1][v]], 1) for v in range(2)]
    o = merged(mm((w56h[...], w56l[...]), split(cat(rows, 0)), NT), 256)
    z = mm(split(cat(o, 1)), (l67h[...], l67l[...]), NT)
    for p in range(2):
        for k in range(4):
            out[pl.ds(p * 4 + k, 64, 8), :] = z[k * 64 : (k + 1) * 64, p * 128 : (p + 1) * 128]


def phase4(x, w7h, w7l, out_real, out_imag):
    o = merged(mm((w7h[...], w7l[...]), split(read_strided(x))), 256)
    for ref, part in zip((out_real, out_imag), o):
        for t in range(2):
            ref[pl.ds(t, 128, 2), :] = rows_of(part, t, 128)


PARAMS = pltpu.CompilerParams(vmem_limit_bytes=48 << 20)
HILO512 = [jax.ShapeDtypeStruct((512, 256), BF16)] * 2
HILO256 = [jax.ShapeDtypeStruct((256, 256), BF16)] * 2


def call(kernel, name, out_shape, flops, *args, scratch=None, out_specs=None):
    more = {}
    if scratch is not None:
        in_hbm = pl.BlockSpec(memory_space=pltpu.HBM)
        more = {"in_specs": [in_hbm] * len(args), "scratch_shapes": scratch}
    if out_specs is not None:
        more["out_specs"] = out_specs
    return pl.pallas_call(
        kernel,
        out_shape=out_shape,
        compiler_params=PARAMS,
        cost_estimate=pl.CostEstimate(flops=flops, bytes_accessed=4 << 20, transcendentals=0),
        name=name,
        **more,
    )(*args)


def on_device(state_real, state_imag, gate_real, gate_imag):
    shape = state_real.shape
    sr, si, gr, gi = (
        pltpu.with_memory_space_constraint(a, pltpu.HBM)
        for a in (
            state_real.reshape(16, 16, 128), state_imag.reshape(16, 16, 128),
            gate_real.reshape(3072, 128), gate_imag.reshape(3072, 128),
        )
    )
    rows = jax.ShapeDtypeStruct((512, 128), F32)
    blocks = jax.ShapeDtypeStruct((16, 2, 2, 8, 128), F32)

    def far(x):
        return lax.all_to_all(x.reshape(16, 32, 128), "far", 0, 0, tiled=True)

    def near(x):
        x = lax.all_to_all(x.reshape(64, 8, 128), "near", 0, 0, tiled=True)
        return x.reshape(512, 128)

    x = call(
        phase0, "phase0", jax.ShapeDtypeStruct((16, 2, 16, 128), F32), 1 << 20, sr, si,
        scratch=[pltpu.VMEM((16, 16, 128), F32)] * 2 + [pltpu.SemaphoreType.DMA((2,))],
    )
    gates = [pltpu.VMEM((3072, 128), F32)] * 2 + [pltpu.SemaphoreType.DMA((2,))]
    x = far(x)
    first = call(
        prepare_first, "prepare_first", HILO256 + HILO512 + HILO256 + HILO512 + HILO512, 1200 << 20,
        gr, gi, scratch=gates,
    )
    x = near(call(phase1, "phase1", rows, 200 << 20, x.reshape(16, 2, 16, 128), *first[:6]))
    x = far(call(phase2, "phase2", blocks, 200 << 20, x, *first[6:]))
    second = call(
        prepare_second, "prepare_second", HILO512 + HILO512 + HILO256 + HILO512, 1600 << 20,
        gr, gi, scratch=gates,
    )
    x = x.reshape(16, 2, 2, 8, 128)
    x = near(call(phase3, "phase3", rows, 200 << 20, x, *second[:6]))
    flat = jax.ShapeDtypeStruct((256, 128), F32)
    real, imag = call(phase4, "phase4", [flat, flat], 200 << 20, x, *second[6:])
    return real.reshape(shape), imag.reshape(shape)


def solution(mesh):
    spec = P("far", "near", None, None, None)
    return jax.shard_map(
        on_device,
        mesh=mesh,
        in_specs=(spec, spec, P(), P()),
        out_specs=(spec, spec),
        check_vma=False,
    )
```

```python
import functools

import jax
import jax.numpy as jnp
from jax import lax
from jax.experimental import pallas as pl
from jax.experimental.pallas import tpu as pltpu
from jax.sharding import PartitionSpec as P

F32, BF16 = jnp.float32, jnp.bfloat16
NN = (((1,), (0,)), ((), ()))
NT = (((1,), (1,)), ((), ()))


def split(x):
    hi = x.astype(BF16)
    return hi, (x - hi.astype(F32)).astype(BF16)


def mm(a, b, dims=NN):
    dot = functools.partial(lax.dot_general, dimension_numbers=dims, preferred_element_type=F32)
    return dot(a[0], b[0]) + (dot(a[0], b[1]) + dot(a[1], b[0]))


def cat(parts, axis):
    return jnp.concatenate(parts, axis)


def rows_of(x, n, count):
    return x[n * count : (n + 1) * count]


def merged(r, n):
    k = r.shape[1] // 2
    return r[:n, :k] - r[n:, k:], r[n:, :k] + r[:n, k:]


def big(real, imag):
    return cat([cat([real, -imag], 1), cat([imag, real], 1)], 0)


def lane_bit(shape, stride):
    return (lax.broadcasted_iota(jnp.int32, shape, 1) // stride) % 2 == 0


def swap(a, b, stride):
    even, lanes = lane_bit(a.shape, stride), a.shape[1]
    return (
        jnp.where(even, a, pltpu.roll(b, stride, 1)),
        jnp.where(even, pltpu.roll(a, lanes - stride, 1), b),
    )


def selector(bit):
    i = lax.broadcasted_iota(jnp.int32, (128, 128), 0)
    j = lax.broadcasted_iota(jnp.int32, (128, 128), 1)
    low, top = i % (1 << bit), i // 64
    mid = (i % 64) // (1 << bit)
    return jnp.where(j == mid * (2 << bit) + top * (1 << bit) + low, 1.0, 0.0).astype(BF16)


def columns_moved(x, sel):
    dot = functools.partial(lax.dot_general, dimension_numbers=NT, preferred_element_type=F32)
    hi, lo = split(x)
    return dot(hi, sel) + dot(lo, sel)


def gate(ref, at):
    return ref[pl.ds(at * 128, 128), :]


def odd_even(ref, at):
    return cat([ref[pl.ds(at * 128 + t, 64, 2), :] for t in range(2)], 0)


def both(read, refs, at):
    return cat([read(ref, at) for ref in refs], 0)


def big_of(x):
    n = x.shape[0] // 2
    return tuple(big(a[:n], a[n:]) for a in split(x))


def product(a, b):
    return mm(big_of(a), split(b))


def combined(c, diagonals):
    x = cat([cat([diagonals[t, p] for p in range(2)], 0) for t in range(2)], 1)
    w = mm(big_of(c), split(x))
    return cat([w[p * 128 : (p + 1) * 128, t * 256 : (t + 1) * 256] for p in range(2) for t in range(2)], 0)


def rows_gate(m, c):
    left, diagonals = lane_bit((64, 128), 64), {}
    for p in range(2):
        for t in range(2):
            x = rows_of(m, p * 2 + t, 64)
            y = pltpu.roll(x, 64, 1)
            blocks = [
                cat([jnp.where(left, up, 0.0), jnp.where(left, 0.0, down)], 0)
                for up, down in ((x, y), (y, x))
            ]
            diagonals[t, p] = cat(blocks, 1)
    return combined(c, diagonals)


def put(refs, x):
    refs[0][...], refs[1][...] = split(x)


def prepare(gr, gi, *rest):
    outs, (vr, vi, sems) = [rest[k : k + 2] for k in range(0, 20, 2)], rest[20:]
    l01, m0, c0, l25, w12, w3, w4, w56, l67, w7 = outs
    refs = (vr, vi)
    copies = []
    for s in range(8):
        at = pl.ds(s * 384, 384)
        copies.append(
            [pltpu.make_async_copy(a.at[at], b.at[at], sems.at[s, p]) for p, (a, b) in enumerate(((gr, vr), (gi, vi)))]
        )
        for copy in copies[s]:
            copy.start()

    def ready(s):
        for copy in copies[s]:
            copy.wait()

    sel, second = selector(0), selector(1)
    ready(0)
    put(m0, both(odd_even, refs, 1))
    put(c0, both(gate, refs, 2))
    ready(1)
    put(l01, product(both(gate, refs, 3), both(gate, refs, 0)))
    ready(2)
    moved = columns_moved(
        cat([both(odd_even, refs, 4), both(odd_even, refs, 7), both(gate, refs, 6)], 0), sel
    )
    w1 = rows_gate(rows_of(moved, 0, 256), both(gate, refs, 5))
    w2 = rows_gate(rows_of(moved, 1, 256), both(odd_even, refs, 8))
    put(w12, product(w2, w1))
    ready(3)
    put(w3, rows_gate(columns_moved(both(odd_even, refs, 10), second), both(gate, refs, 11)))
    x = product(both(gate, refs, 9), rows_of(moved, 2, 256))
    ready(4)
    ready(5)
    y = product(both(odd_even, refs, 15), both(gate, refs, 12))
    put(l25, product(y, x))
    ready(6)
    ready(7)
    moved = columns_moved(
        cat([both(odd_even, refs, k) for k in (13, 16, 19, 22)] + [both(gate, refs, 18)], 0), sel
    )
    put(w4, rows_gate(rows_of(moved, 0, 256), both(gate, refs, 14)))
    w5 = rows_gate(rows_of(moved, 1, 256), both(gate, refs, 17))
    w6 = rows_gate(rows_of(moved, 2, 256), both(odd_even, refs, 20))
    put(w56, product(w6, w5))
    put(l67, product(both(gate, refs, 21), rows_of(moved, 4, 256)))
    w = rows_gate(rows_of(moved, 3, 256), both(gate, refs, 23))
    put(w7, cat([columns_moved(w[:, :128], sel), columns_moved(w[:, 128:], sel)], 1))


def read_big(h, l):
    return tuple(big(a[:128], a[128:]) for a in (h[...], l[...]))


def read_blocks(ref):
    return cat(
        [cat([ref[:, p, t].reshape(128, 128) for t in range(2)], 0) for p in range(2)], 1
    )


def read_strided(ref):
    return cat(
        [cat([ref[pl.ds(p * 4 + o, 64, 8), :] for o in range(4)], 0) for p in range(2)], 1
    )


def phase0(sr, si, out, vr, vi, sems):
    pairs = [(sr, vr), (si, vi)]
    copies = [pltpu.make_async_copy(a, b, sems.at[p]) for p, (a, b) in enumerate(pairs)]
    for copy in copies:
        copy.start()
    for p, copy in enumerate(copies):
        copy.wait()
        out[:, p] = pairs[p][1][...]


def phase1(x, l01h, l01l, m0h, m0l, c0h, c0l, l25h, l25l, out):
    y = cat([x[:, p].reshape(256, 128) for p in range(2)], 1)
    y = mm(split(y), read_big(l01h, l01l), NT)
    half = lambda a, k: a[:, k * 128 : (k + 1) * 128]
    y = cat([cat([rows_of(half(y, p), h, 128) for h in range(2)], 1) for p in range(2)], 0)
    y = mm(read_big(m0h, m0l), split(y))
    rows = [cat([half(rows_of(y, 2 * p + t, 64), h) for t in range(2)], 1) for p in range(2) for h in range(2)]
    y = mm(read_big(c0h, c0l), split(cat(rows, 0)))
    o = [rows_of(y, p, 128) for p in range(2)]
    o = [cat([half(a, 0), half(a, 1)], 0) for a in o]
    u = [swap(o[p][:128], o[p][128:], 1) for p in range(2)]
    rows = [u[p][v] for p in range(2) for v in range(2)]
    u = cat([cat([rows_of(r, f, 64) for r in rows], 0) for f in range(2)], 1)
    v = mm(read_big(l25h, l25l), split(u))
    for p in range(2):
        for f in range(2):
            block = v[p * 128 : (p + 1) * 128, f * 128 : (f + 1) * 128]
            for t, y in enumerate(swap(block[:64], block[64:], 1)):
                out[pl.ds(p * 4 + t * 2 + f, 64, 8), :] = y


def phase2(x, w12h, w12l, w3h, w3l, out):
    o = merged(mm((w12h[...], w12l[...]), split(read_strided(x))), 256)
    u = [swap(o[p][:128], o[p][128:], 1) for p in range(2)]
    rows = [u[p][v] for p in range(2) for v in range(2)]
    u = cat([cat([rows_of(r, a, 64) for a in range(2)], 1) for r in rows], 0)
    o = merged(mm((w3h[...], w3l[...]), split(u), NT), 256)
    for p in range(2):
        for t in range(2):
            out[:, p, t] = rows_of(o[p], t, 128).reshape(16, 8, 128)


def phase3(x, w4h, w4l, w56h, w56l, l67h, l67l, out):
    o = merged(mm((w4h[...], w4l[...]), split(read_blocks(x))), 256)
    rows = []
    for p in range(2):
        pairs = [swap(rows_of(o[p], 2 * t, 64), rows_of(o[p], 2 * t + 1, 64), 64) for t in range(2)]
        rows += [cat([pairs[0][v], pairs[1][v]], 1) for v in range(2)]
    o = merged(mm((w56h[...], w56l[...]), split(cat(rows, 0)), NT), 256)
    z = mm(split(cat(o, 1)), read_big(l67h, l67l), NT)
    for p in range(2):
        for k in range(4):
            out[pl.ds(p * 4 + k, 64, 8), :] = z[k * 64 : (k + 1) * 64, p * 128 : (p + 1) * 128]


def phase4(x, w7h, w7l, out_real, out_imag):
    o = merged(mm((w7h[...], w7l[...]), split(read_strided(x))), 256)
    for ref, part in zip((out_real, out_imag), o):
        for t in range(2):
            ref[pl.ds(t, 128, 2), :] = rows_of(part, t, 128)


PARAMS = pltpu.CompilerParams(vmem_limit_bytes=48 << 20)
HILO512 = [jax.ShapeDtypeStruct((512, 256), BF16)] * 2
HILO256 = [jax.ShapeDtypeStruct((256, 128), BF16)] * 2


def call(kernel, name, out_shape, flops, *args, scratch=None, out_specs=None):
    more = {}
    if scratch is not None:
        in_hbm = pl.BlockSpec(memory_space=pltpu.HBM)
        more = {"in_specs": [in_hbm] * len(args), "scratch_shapes": scratch}
    if out_specs is not None:
        more["out_specs"] = out_specs
    return pl.pallas_call(
        kernel,
        out_shape=out_shape,
        compiler_params=PARAMS,
        cost_estimate=pl.CostEstimate(flops=flops, bytes_accessed=4 << 20, transcendentals=0),
        name=name,
        **more,
    )(*args)


def on_device(state_real, state_imag, gate_real, gate_imag):
    shape = state_real.shape
    sr, si, gr, gi = (
        pltpu.with_memory_space_constraint(a, pltpu.HBM)
        for a in (
            state_real.reshape(16, 16, 128), state_imag.reshape(16, 16, 128),
            gate_real.reshape(3072, 128), gate_imag.reshape(3072, 128),
        )
    )
    rows = jax.ShapeDtypeStruct((512, 128), F32)
    blocks = jax.ShapeDtypeStruct((16, 2, 2, 8, 128), F32)

    def far(x):
        return lax.all_to_all(x.reshape(16, 32, 128), "far", 0, 0, tiled=True)

    def near(x):
        x = lax.all_to_all(x.reshape(64, 8, 128), "near", 0, 0, tiled=True)
        return x.reshape(512, 128)

    x = call(
        phase0, "phase0", jax.ShapeDtypeStruct((16, 2, 16, 128), F32), 1 << 20, sr, si,
        scratch=[pltpu.VMEM((16, 16, 128), F32)] * 2 + [pltpu.SemaphoreType.DMA((2,))],
    )
    x = far(x)
    w = call(
        prepare, "prepare",
        HILO256 * 4 + HILO512 * 4 + HILO256 + HILO512, 2400 << 20,
        gr, gi, scratch=[pltpu.VMEM((3072, 128), F32)] * 2 + [pltpu.SemaphoreType.DMA((8, 2))],
    )
    x = near(call(phase1, "phase1", rows, 200 << 20, x.reshape(16, 2, 16, 128), *w[:8]))
    x = far(call(phase2, "phase2", blocks, 200 << 20, x, *w[8:12])).reshape(16, 2, 2, 8, 128)
    x = near(call(phase3, "phase3", rows, 200 << 20, x, *w[12:18]))
    flat = jax.ShapeDtypeStruct((256, 128), F32)
    real, imag = call(phase4, "phase4", [flat, flat], 200 << 20, x, *w[18:])
    return real.reshape(shape), imag.reshape(shape)


def solution(mesh):
    spec = P("far", "near", None, None, None)
    return jax.shard_map(
        on_device,
        mesh=mesh,
        in_specs=(spec, spec, P(), P()),
        out_specs=(spec, spec),
        check_vma=False,
    )
```

```python
import functools

import jax
import jax.numpy as jnp
from jax import lax
from jax.experimental import pallas as pl
from jax.experimental.pallas import tpu as pltpu
from jax.sharding import PartitionSpec as P

F32, BF16 = jnp.float32, jnp.bfloat16
NN = (((1,), (0,)), ((), ()))
NT = (((1,), (1,)), ((), ()))


def split(x):
    hi = x.astype(BF16)
    return hi, (x - hi.astype(F32)).astype(BF16)


def mm(a, b, dims=NN):
    dot = functools.partial(lax.dot_general, dimension_numbers=dims, preferred_element_type=F32)
    return dot(a[0], b[0]) + (dot(a[0], b[1]) + dot(a[1], b[0]))


def mm_rows(a, b, dims=NN, step=128):
    n = a[0].shape[0]
    return cat([mm(tuple(p[k : k + step] for p in a), b, dims) for k in range(0, n, step)], 0)


def cat(parts, axis):
    return jnp.concatenate(parts, axis)


def rows_of(x, n, count):
    return x[n * count : (n + 1) * count]


def merged(r, n):
    k = r.shape[1] // 2
    return r[:n, :k] - r[n:, k:], r[n:, :k] + r[:n, k:]


def applied(h, l, x, dims=NN):
    parts = []
    for k in range(0, 256, 128):
        w = tuple(cat([ref[pl.ds(k, 128), :], ref[pl.ds(256 + k, 128), :]], 0) for ref in (h, l))
        parts.append(merged(mm(w, x, dims), 128))
    return tuple(cat([p[k] for p in parts], 0) for k in range(2))


def big(real, imag):
    return cat([cat([real, -imag], 1), cat([imag, real], 1)], 0)


def lane_bit(shape, stride):
    return (lax.broadcasted_iota(jnp.int32, shape, 1) // stride) % 2 == 0


def swap(a, b, stride):
    even, lanes = lane_bit(a.shape, stride), a.shape[1]
    return (
        jnp.where(even, a, pltpu.roll(b, stride, 1)),
        jnp.where(even, pltpu.roll(a, lanes - stride, 1), b),
    )


def selector(bit):
    i = lax.broadcasted_iota(jnp.int32, (128, 128), 0)
    j = lax.broadcasted_iota(jnp.int32, (128, 128), 1)
    low, top = i % (1 << bit), i // 64
    mid = (i % 64) // (1 << bit)
    return jnp.where(j == mid * (2 << bit) + top * (1 << bit) + low, 1.0, 0.0).astype(BF16)


def columns_moved(x, sel):
    dot = functools.partial(lax.dot_general, dimension_numbers=NT, preferred_element_type=F32)
    hi, lo = split(x)
    return dot(hi, sel) + dot(lo, sel)


def gate(ref, at):
    return ref[pl.ds(at * 128, 128), :]


def odd_even(ref, at):
    return cat([ref[pl.ds(at * 128 + t, 64, 2), :] for t in range(2)], 0)


def both(read, refs, at):
    return cat([read(ref, at) for ref in refs], 0)


def big_of(x):
    n = x.shape[0] // 2
    return tuple(big(a[:n], a[n:]) for a in split(x))


def product(a, b):
    return mm_rows(big_of(a), split(b))


def combined(c, diagonals):
    x = cat([cat([diagonals[t, p] for p in range(2)], 0) for t in range(2)], 1)
    w = mm_rows(big_of(c), split(x))
    return cat([w[p * 128 : (p + 1) * 128, t * 256 : (t + 1) * 256] for p in range(2) for t in range(2)], 0)


def rows_gate(m, c):
    left, diagonals = lane_bit((64, 128), 64), {}
    for p in range(2):
        for t in range(2):
            x = rows_of(m, p * 2 + t, 64)
            y = pltpu.roll(x, 64, 1)
            blocks = [
                cat([jnp.where(left, up, 0.0), jnp.where(left, 0.0, down)], 0)
                for up, down in ((x, y), (y, x))
            ]
            diagonals[t, p] = cat(blocks, 1)
    return combined(c, diagonals)


def put(refs, x):
    refs[0][...], refs[1][...] = split(x)


def prepare(gr, gi, *rest):
    outs, (vr, vi, sems) = [rest[k : k + 2] for k in range(0, 20, 2)], rest[20:]
    l01, m0, c0, l25, w12, w3, w4, w56, l67, w7 = outs
    refs = (vr, vi)
    copies = []
    for s in range(8):
        at = pl.ds(s * 384, 384)
        copies.append(
            [pltpu.make_async_copy(a.at[at], b.at[at], sems.at[s, p]) for p, (a, b) in enumerate(((gr, vr), (gi, vi)))]
        )
        for copy in copies[s]:
            copy.start()

    def ready(s):
        for copy in copies[s]:
            copy.wait()

    sel, second = selector(0), selector(1)
    ready(0)
    put(m0, both(odd_even, refs, 1))
    put(c0, both(gate, refs, 2))
    ready(1)
    put(l01, product(both(gate, refs, 3), both(gate, refs, 0)))
    ready(2)
    moved = columns_moved(
        cat([both(odd_even, refs, 4), both(odd_even, refs, 7), both(gate, refs, 6)], 0), sel
    )
    w1 = rows_gate(rows_of(moved, 0, 256), both(gate, refs, 5))
    w2 = rows_gate(rows_of(moved, 1, 256), both(odd_even, refs, 8))
    put(w12, product(w2, w1))
    ready(3)
    put(w3, rows_gate(columns_moved(both(odd_even, refs, 10), second), both(gate, refs, 11)))
    x = product(both(gate, refs, 9), rows_of(moved, 2, 256))
    ready(4)
    ready(5)
    y = product(both(odd_even, refs, 15), both(gate, refs, 12))
    put(l25, product(y, x))
    ready(6)
    ready(7)
    moved = columns_moved(
        cat([both(odd_even, refs, k) for k in (13, 16, 19, 22)] + [both(gate, refs, 18)], 0), sel
    )
    put(w4, rows_gate(rows_of(moved, 0, 256), both(gate, refs, 14)))
    w5 = rows_gate(rows_of(moved, 1, 256), both(gate, refs, 17))
    w6 = rows_gate(rows_of(moved, 2, 256), both(odd_even, refs, 20))
    put(w56, product(w6, w5))
    put(l67, product(both(gate, refs, 21), rows_of(moved, 4, 256)))
    w = rows_gate(rows_of(moved, 3, 256), both(gate, refs, 23))
    put(w7, cat([columns_moved(w[:, :128], sel), columns_moved(w[:, 128:], sel)], 1))


def read_big(h, l):
    return tuple(big(a[:128], a[128:]) for a in (h[...], l[...]))


def read_blocks(ref):
    return cat(
        [cat([ref[:, p, t].reshape(128, 128) for t in range(2)], 0) for p in range(2)], 1
    )


def read_strided(ref):
    return cat(
        [cat([ref[pl.ds(p * 4 + o, 64, 8), :] for o in range(4)], 0) for p in range(2)], 1
    )


def phase0(sr, si, out, vr, vi, sems):
    pairs = [(sr, vr), (si, vi)]
    copies = [pltpu.make_async_copy(a, b, sems.at[p]) for p, (a, b) in enumerate(pairs)]
    for copy in copies:
        copy.start()
    for p, copy in enumerate(copies):
        copy.wait()
        out[:, p] = pairs[p][1][...]


def phase1(x, l01h, l01l, m0h, m0l, c0h, c0l, l25h, l25l, out):
    y = cat([x[:, p].reshape(256, 128) for p in range(2)], 1)
    y = mm_rows(split(y), read_big(l01h, l01l), NT)
    half = lambda a, k: a[:, k * 128 : (k + 1) * 128]
    y = cat([cat([rows_of(half(y, p), h, 128) for h in range(2)], 1) for p in range(2)], 0)
    y = mm_rows(read_big(m0h, m0l), split(y))
    rows = [cat([half(rows_of(y, 2 * p + t, 64), h) for t in range(2)], 1) for p in range(2) for h in range(2)]
    y = mm_rows(read_big(c0h, c0l), split(cat(rows, 0)))
    o = [rows_of(y, p, 128) for p in range(2)]
    o = [cat([half(a, 0), half(a, 1)], 0) for a in o]
    u = [swap(o[p][:128], o[p][128:], 1) for p in range(2)]
    rows = [u[p][v] for p in range(2) for v in range(2)]
    u = cat([cat([rows_of(r, f, 64) for r in rows], 0) for f in range(2)], 1)
    v = mm_rows(read_big(l25h, l25l), split(u))
    for p in range(2):
        for f in range(2):
            block = v[p * 128 : (p + 1) * 128, f * 128 : (f + 1) * 128]
            for t, y in enumerate(swap(block[:64], block[64:], 1)):
                out[pl.ds(p * 4 + t * 2 + f, 64, 8), :] = y


def phase2(x, w12h, w12l, w3h, w3l, out):
    o = applied(w12h, w12l, split(read_strided(x)))
    u = [swap(o[p][:128], o[p][128:], 1) for p in range(2)]
    rows = [u[p][v] for p in range(2) for v in range(2)]
    u = cat([cat([rows_of(r, a, 64) for a in range(2)], 1) for r in rows], 0)
    o = applied(w3h, w3l, split(u), NT)
    for p in range(2):
        for t in range(2):
            out[:, p, t] = rows_of(o[p], t, 128).reshape(16, 8, 128)


def phase3(x, w4h, w4l, w56h, w56l, l67h, l67l, out):
    o = applied(w4h, w4l, split(read_blocks(x)))
    rows = []
    for p in range(2):
        pairs = [swap(rows_of(o[p], 2 * t, 64), rows_of(o[p], 2 * t + 1, 64), 64) for t in range(2)]
        rows += [cat([pairs[0][v], pairs[1][v]], 1) for v in range(2)]
    o = applied(w56h, w56l, split(cat(rows, 0)), NT)
    z = mm_rows(split(cat(o, 1)), read_big(l67h, l67l), NT)
    for p in range(2):
        for k in range(4):
            out[pl.ds(p * 4 + k, 64, 8), :] = z[k * 64 : (k + 1) * 64, p * 128 : (p + 1) * 128]


def phase4(x, w7h, w7l, out_real, out_imag):
    o = applied(w7h, w7l, split(read_strided(x)))
    for ref, part in zip((out_real, out_imag), o):
        for t in range(2):
            ref[pl.ds(t, 128, 2), :] = rows_of(part, t, 128)


PARAMS = pltpu.CompilerParams(vmem_limit_bytes=48 << 20)
HILO512 = [jax.ShapeDtypeStruct((512, 256), BF16)] * 2
HILO256 = [jax.ShapeDtypeStruct((256, 128), BF16)] * 2


def call(kernel, name, out_shape, flops, *args, scratch=None, out_specs=None):
    more = {}
    if scratch is not None:
        in_hbm = pl.BlockSpec(memory_space=pltpu.HBM)
        more = {"in_specs": [in_hbm] * len(args), "scratch_shapes": scratch}
    if out_specs is not None:
        more["out_specs"] = out_specs
    return pl.pallas_call(
        kernel,
        out_shape=out_shape,
        compiler_params=PARAMS,
        cost_estimate=pl.CostEstimate(flops=flops, bytes_accessed=4 << 20, transcendentals=0),
        name=name,
        **more,
    )(*args)


def on_device(state_real, state_imag, gate_real, gate_imag):
    shape = state_real.shape
    sr, si, gr, gi = (
        pltpu.with_memory_space_constraint(a, pltpu.HBM)
        for a in (
            state_real.reshape(16, 16, 128), state_imag.reshape(16, 16, 128),
            gate_real.reshape(3072, 128), gate_imag.reshape(3072, 128),
        )
    )
    rows = jax.ShapeDtypeStruct((512, 128), F32)
    blocks = jax.ShapeDtypeStruct((16, 2, 2, 8, 128), F32)

    def far(x):
        return lax.all_to_all(x.reshape(16, 32, 128), "far", 0, 0, tiled=True)

    def near(x):
        x = lax.all_to_all(x.reshape(64, 8, 128), "near", 0, 0, tiled=True)
        return x.reshape(512, 128)

    x = call(
        phase0, "phase0", jax.ShapeDtypeStruct((16, 2, 16, 128), F32), 1 << 20, sr, si,
        scratch=[pltpu.VMEM((16, 16, 128), F32)] * 2 + [pltpu.SemaphoreType.DMA((2,))],
    )
    x = far(x)
    w = call(
        prepare, "prepare",
        HILO256 * 4 + HILO512 * 4 + HILO256 + HILO512, 2400 << 20,
        gr, gi, scratch=[pltpu.VMEM((3072, 128), F32)] * 2 + [pltpu.SemaphoreType.DMA((8, 2))],
    )
    x = near(call(phase1, "phase1", rows, 200 << 20, x.reshape(16, 2, 16, 128), *w[:8]))
    x = far(call(phase2, "phase2", blocks, 200 << 20, x, *w[8:12])).reshape(16, 2, 2, 8, 128)
    x = near(call(phase3, "phase3", rows, 200 << 20, x, *w[12:18]))
    flat = jax.ShapeDtypeStruct((256, 128), F32)
    real, imag = call(phase4, "phase4", [flat, flat], 200 << 20, x, *w[18:])
    return real.reshape(shape), imag.reshape(shape)


def solution(mesh):
    spec = P("far", "near", None, None, None)
    return jax.shard_map(
        on_device,
        mesh=mesh,
        in_specs=(spec, spec, P(), P()),
        out_specs=(spec, spec),
        check_vma=False,
    )
```

```python
import functools

import jax
import jax.numpy as jnp
from jax import lax
from jax.experimental import pallas as pl
from jax.experimental.pallas import tpu as pltpu
from jax.sharding import PartitionSpec as P

F32, BF16 = jnp.float32, jnp.bfloat16
NN = (((1,), (0,)), ((), ()))
NT = (((1,), (1,)), ((), ()))


def split(x):
    hi = x.astype(BF16)
    return hi, (x - hi.astype(F32)).astype(BF16)


def mm(a, b, dims=NN):
    dot = functools.partial(lax.dot_general, dimension_numbers=dims, preferred_element_type=F32)
    return dot(a[0], b[0]) + (dot(a[0], b[1]) + dot(a[1], b[0]))


def mm_rows(a, b, dims=NN, step=128):
    n = a[0].shape[0]
    return cat([mm(tuple(p[k : k + step] for p in a), b, dims) for k in range(0, n, step)], 0)


def cat(parts, axis):
    return jnp.concatenate(parts, axis)


def rows_of(x, n, count):
    return x[n * count : (n + 1) * count]


def merged(r, n):
    k = r.shape[1] // 2
    return r[:n, :k] - r[n:, k:], r[n:, :k] + r[:n, k:]


def applied(h, l, x, dims=NN):
    parts = []
    for k in range(0, 256, 128):
        w = tuple(cat([ref[pl.ds(k, 128), :], ref[pl.ds(256 + k, 128), :]], 0) for ref in (h, l))
        parts.append(merged(mm(w, x, dims), 128))
    return tuple(cat([p[k] for p in parts], 0) for k in range(2))


def big(real, imag):
    return cat([cat([real, -imag], 1), cat([imag, real], 1)], 0)


def lane_bit(shape, stride):
    return (lax.broadcasted_iota(jnp.int32, shape, 1) // stride) % 2 == 0


def swap(a, b, stride):
    even, lanes = lane_bit(a.shape, stride), a.shape[1]
    return (
        jnp.where(even, a, pltpu.roll(b, stride, 1)),
        jnp.where(even, pltpu.roll(a, lanes - stride, 1), b),
    )


def selector(bit):
    i = lax.broadcasted_iota(jnp.int32, (128, 128), 0)
    j = lax.broadcasted_iota(jnp.int32, (128, 128), 1)
    low, top = i % (1 << bit), i // 64
    mid = (i % 64) // (1 << bit)
    return jnp.where(j == mid * (2 << bit) + top * (1 << bit) + low, 1.0, 0.0).astype(BF16)


def columns_moved(x, sel):
    dot = functools.partial(lax.dot_general, dimension_numbers=NT, preferred_element_type=F32)
    hi, lo = split(x)
    return dot(hi, sel) + dot(lo, sel)


def gate(ref, at):
    return ref[pl.ds(at * 128, 128), :]


def odd_even(ref, at):
    return cat([ref[pl.ds(at * 128 + t, 64, 2), :] for t in range(2)], 0)


def both(read, refs, at):
    return cat([read(ref, at) for ref in refs], 0)


def big_of(x):
    n = x.shape[0] // 2
    return tuple(big(a[:n], a[n:]) for a in split(x))


def product(a, b):
    return mm_rows(big_of(a), split(b))


def combined(c, diagonals):
    x = cat([cat([diagonals[t, p] for p in range(2)], 0) for t in range(2)], 1)
    w = mm_rows(big_of(c), split(x))
    return cat([w[p * 128 : (p + 1) * 128, t * 256 : (t + 1) * 256] for p in range(2) for t in range(2)], 0)


def rows_gate(m, c):
    left, diagonals = lane_bit((64, 128), 64), {}
    for p in range(2):
        for t in range(2):
            x = rows_of(m, p * 2 + t, 64)
            y = pltpu.roll(x, 64, 1)
            blocks = [
                cat([jnp.where(left, up, 0.0), jnp.where(left, 0.0, down)], 0)
                for up, down in ((x, y), (y, x))
            ]
            diagonals[t, p] = cat(blocks, 1)
    return combined(c, diagonals)


def put(refs, x):
    refs[0][...], refs[1][...] = split(x)


def prepare(gr, gi, *rest):
    outs, (vr, vi, sems) = [rest[k : k + 2] for k in range(0, 20, 2)], rest[20:]
    l01, m0, c0, l25, w12, w3, w4, w56, l67, w7 = outs
    refs = (vr, vi)
    copies = []
    for s in range(8):
        at = pl.ds(s * 384, 384)
        copies.append(
            [pltpu.make_async_copy(a.at[at], b.at[at], sems.at[s, p]) for p, (a, b) in enumerate(((gr, vr), (gi, vi)))]
        )
        for copy in copies[s]:
            copy.start()

    def ready(s):
        for copy in copies[s]:
            copy.wait()

    sel, second = selector(0), selector(1)
    ready(0)
    put(m0, both(odd_even, refs, 1))
    put(c0, both(gate, refs, 2))
    ready(1)
    put(l01, turned(product(both(gate, refs, 3), both(gate, refs, 0))))
    ready(2)
    moved = columns_moved(
        cat([both(odd_even, refs, 4), both(odd_even, refs, 7), both(gate, refs, 6)], 0), sel
    )
    w1 = rows_gate(rows_of(moved, 0, 256), both(gate, refs, 5))
    w2 = rows_gate(rows_of(moved, 1, 256), both(odd_even, refs, 8))
    put(w12, product(w2, w1))
    ready(3)
    put(w3, rows_gate(columns_moved(both(odd_even, refs, 10), second), both(gate, refs, 11)))
    x = product(both(gate, refs, 9), rows_of(moved, 2, 256))
    ready(4)
    ready(5)
    y = product(both(odd_even, refs, 15), both(gate, refs, 12))
    put(l25, product(y, x))
    ready(6)
    ready(7)
    moved = columns_moved(
        cat([both(odd_even, refs, k) for k in (13, 16, 19, 22)] + [both(gate, refs, 18)], 0), sel
    )
    put(w4, rows_gate(rows_of(moved, 0, 256), both(gate, refs, 14)))
    w5 = rows_gate(rows_of(moved, 1, 256), both(gate, refs, 17))
    w6 = rows_gate(rows_of(moved, 2, 256), both(odd_even, refs, 20))
    put(w56, product(w6, w5))
    put(l67, turned(product(both(gate, refs, 21), rows_of(moved, 4, 256))))
    w = rows_gate(rows_of(moved, 3, 256), both(gate, refs, 23))
    put(w7, cat([columns_moved(w[:, :128], sel), columns_moved(w[:, 128:], sel)], 1))


def turned(x):
    n = x.shape[0] // 2
    return cat([x[:n].T, x[n:].T], 0)


def read_turned(h, l):
    return tuple(big(a[:128], -a[128:]) for a in (h[...], l[...]))


def read_big(h, l):
    return tuple(big(a[:128], a[128:]) for a in (h[...], l[...]))


def read_blocks(ref):
    return cat(
        [cat([ref[:, p, t].reshape(128, 128) for t in range(2)], 0) for p in range(2)], 1
    )


def read_strided(ref):
    return cat(
        [cat([ref[pl.ds(p * 4 + o, 64, 8), :] for o in range(4)], 0) for p in range(2)], 1
    )


def phase0(sr, si, out, vr, vi, sems):
    pairs = [(sr, vr), (si, vi)]
    copies = [pltpu.make_async_copy(a, b, sems.at[p]) for p, (a, b) in enumerate(pairs)]
    for copy in copies:
        copy.start()
    for p, copy in enumerate(copies):
        copy.wait()
        out[:, p] = pairs[p][1][...]


def phase1(x, l01h, l01l, m0h, m0l, c0h, c0l, l25h, l25l, out):
    y = cat([x[:, p].reshape(256, 128) for p in range(2)], 1)
    y = mm_rows(split(y), read_turned(l01h, l01l))
    half = lambda a, k: a[:, k * 128 : (k + 1) * 128]
    y = cat([cat([rows_of(half(y, p), h, 128) for h in range(2)], 1) for p in range(2)], 0)
    y = mm_rows(read_big(m0h, m0l), split(y))
    rows = [cat([half(rows_of(y, 2 * p + t, 64), h) for t in range(2)], 1) for p in range(2) for h in range(2)]
    y = mm_rows(read_big(c0h, c0l), split(cat(rows, 0)))
    o = [rows_of(y, p, 128) for p in range(2)]
    o = [cat([half(a, 0), half(a, 1)], 0) for a in o]
    u = [swap(o[p][:128], o[p][128:], 1) for p in range(2)]
    rows = [u[p][v] for p in range(2) for v in range(2)]
    u = cat([cat([rows_of(r, f, 64) for r in rows], 0) for f in range(2)], 1)
    v = mm_rows(read_big(l25h, l25l), split(u))
    for p in range(2):
        for f in range(2):
            block = v[p * 128 : (p + 1) * 128, f * 128 : (f + 1) * 128]
            for t, y in enumerate(swap(block[:64], block[64:], 1)):
                out[pl.ds(p * 4 + t * 2 + f, 64, 8), :] = y


def phase2(x, w12h, w12l, w3h, w3l, out):
    o = applied(w12h, w12l, split(read_strided(x)))
    u = [swap(o[p][:128], o[p][128:], 1) for p in range(2)]
    rows = [u[p][v] for p in range(2) for v in range(2)]
    u = cat([cat([rows_of(r, a, 64) for a in range(2)], 1) for r in rows], 0)
    o = applied(w3h, w3l, split(u), NT)
    for p in range(2):
        for t in range(2):
            out[:, p, t] = rows_of(o[p], t, 128).reshape(16, 8, 128)


def phase3(x, w4h, w4l, w56h, w56l, l67h, l67l, out):
    o = applied(w4h, w4l, split(read_blocks(x)))
    rows = []
    for p in range(2):
        pairs = [swap(rows_of(o[p], 2 * t, 64), rows_of(o[p], 2 * t + 1, 64), 64) for t in range(2)]
        rows += [cat([pairs[0][v], pairs[1][v]], 1) for v in range(2)]
    o = applied(w56h, w56l, split(cat(rows, 0)), NT)
    z = mm_rows(split(cat(o, 1)), read_turned(l67h, l67l))
    for p in range(2):
        for k in range(4):
            out[pl.ds(p * 4 + k, 64, 8), :] = z[k * 64 : (k + 1) * 64, p * 128 : (p + 1) * 128]


def phase4(x, w7h, w7l, out_real, out_imag):
    o = applied(w7h, w7l, split(read_strided(x)))
    for ref, part in zip((out_real, out_imag), o):
        for t in range(2):
            ref[pl.ds(t, 128, 2), :] = rows_of(part, t, 128)


PARAMS = pltpu.CompilerParams(vmem_limit_bytes=48 << 20)
HILO512 = [jax.ShapeDtypeStruct((512, 256), BF16)] * 2
HILO256 = [jax.ShapeDtypeStruct((256, 128), BF16)] * 2


def call(kernel, name, out_shape, flops, *args, scratch=None, out_specs=None):
    more = {}
    if scratch is not None:
        in_hbm = pl.BlockSpec(memory_space=pltpu.HBM)
        more = {"in_specs": [in_hbm] * len(args), "scratch_shapes": scratch}
    if out_specs is not None:
        more["out_specs"] = out_specs
    return pl.pallas_call(
        kernel,
        out_shape=out_shape,
        compiler_params=PARAMS,
        cost_estimate=pl.CostEstimate(flops=flops, bytes_accessed=4 << 20, transcendentals=0),
        name=name,
        **more,
    )(*args)


def on_device(state_real, state_imag, gate_real, gate_imag):
    shape = state_real.shape
    sr, si, gr, gi = (
        pltpu.with_memory_space_constraint(a, pltpu.HBM)
        for a in (
            state_real.reshape(16, 16, 128), state_imag.reshape(16, 16, 128),
            gate_real.reshape(3072, 128), gate_imag.reshape(3072, 128),
        )
    )
    rows = jax.ShapeDtypeStruct((512, 128), F32)
    blocks = jax.ShapeDtypeStruct((16, 2, 2, 8, 128), F32)

    def far(x):
        return lax.all_to_all(x.reshape(16, 32, 128), "far", 0, 0, tiled=True)

    def near(x):
        x = lax.all_to_all(x.reshape(64, 8, 128), "near", 0, 0, tiled=True)
        return x.reshape(512, 128)

    x = call(
        phase0, "phase0", jax.ShapeDtypeStruct((16, 2, 16, 128), F32), 1 << 20, sr, si,
        scratch=[pltpu.VMEM((16, 16, 128), F32)] * 2 + [pltpu.SemaphoreType.DMA((2,))],
    )
    x = far(x)
    w = call(
        prepare, "prepare",
        HILO256 * 4 + HILO512 * 4 + HILO256 + HILO512, 2400 << 20,
        gr, gi, scratch=[pltpu.VMEM((3072, 128), F32)] * 2 + [pltpu.SemaphoreType.DMA((8, 2))],
    )
    x = near(call(phase1, "phase1", rows, 200 << 20, x.reshape(16, 2, 16, 128), *w[:8]))
    x = far(call(phase2, "phase2", blocks, 200 << 20, x, *w[8:12])).reshape(16, 2, 2, 8, 128)
    x = near(call(phase3, "phase3", rows, 200 << 20, x, *w[12:18]))
    flat = jax.ShapeDtypeStruct((256, 128), F32)
    real, imag = call(phase4, "phase4", [flat, flat], 200 << 20, x, *w[18:])
    return real.reshape(shape), imag.reshape(shape)


def solution(mesh):
    spec = P("far", "near", None, None, None)
    return jax.shard_map(
        on_device,
        mesh=mesh,
        in_specs=(spec, spec, P(), P()),
        out_specs=(spec, spec),
        check_vma=False,
    )
```

```python
import functools

import jax
import jax.numpy as jnp
from jax import lax
from jax.experimental import pallas as pl
from jax.experimental.pallas import tpu as pltpu
from jax.sharding import PartitionSpec as P

F32, BF16 = jnp.float32, jnp.bfloat16
NN = (((1,), (0,)), ((), ()))
NT = (((1,), (1,)), ((), ()))


def split(x):
    hi = x.astype(BF16)
    return hi, (x - hi.astype(F32)).astype(BF16)


def mm(a, b, dims=NN):
    dot = functools.partial(lax.dot_general, dimension_numbers=dims, preferred_element_type=F32)
    return dot(a[0], b[0]) + (dot(a[0], b[1]) + dot(a[1], b[0]))


def mm_rows(a, b, dims=NN, step=128):
    n = a[0].shape[0]
    return cat([mm(tuple(p[k : k + step] for p in a), b, dims) for k in range(0, n, step)], 0)


def cat(parts, axis):
    return jnp.concatenate(parts, axis)


def rows_of(x, n, count):
    return x[n * count : (n + 1) * count]


def merged(r, n):
    k = r.shape[1] // 2
    return r[:n, :k] - r[n:, k:], r[n:, :k] + r[:n, k:]


def applied(h, l, x, dims=NN):
    parts = []
    for k in range(0, 256, 128):
        w = tuple(cat([ref[pl.ds(k, 128), :], ref[pl.ds(256 + k, 128), :]], 0) for ref in (h, l))
        parts.append(merged(mm(w, x, dims), 128))
    return tuple(cat([p[k] for p in parts], 0) for k in range(2))


def big(real, imag):
    return cat([cat([real, -imag], 1), cat([imag, real], 1)], 0)


def lane_bit(shape, stride):
    return (lax.broadcasted_iota(jnp.int32, shape, 1) // stride) % 2 == 0


def swap(a, b, stride):
    even, lanes = lane_bit(a.shape, stride), a.shape[1]
    return (
        jnp.where(even, a, pltpu.roll(b, stride, 1)),
        jnp.where(even, pltpu.roll(a, lanes - stride, 1), b),
    )


def selector(bit):
    i = lax.broadcasted_iota(jnp.int32, (128, 128), 0)
    j = lax.broadcasted_iota(jnp.int32, (128, 128), 1)
    low, top = i % (1 << bit), i // 64
    mid = (i % 64) // (1 << bit)
    return jnp.where(j == mid * (2 << bit) + top * (1 << bit) + low, 1.0, 0.0).astype(BF16)


def columns_moved(x, sel):
    dot = functools.partial(lax.dot_general, dimension_numbers=NT, preferred_element_type=F32)
    hi, lo = split(x)
    return dot(hi, sel) + dot(lo, sel)


def gate(ref, at):
    return ref[pl.ds(at * 128, 128), :]


def odd_even(ref, at):
    return cat([ref[pl.ds(at * 128 + t, 64, 2), :] for t in range(2)], 0)


def both(read, refs, at):
    return cat([read(ref, at) for ref in refs], 0)


def big_of(x):
    n = x.shape[0] // 2
    return tuple(big(a[:n], a[n:]) for a in split(x))


def product(a, b):
    return mm_rows(big_of(a), split(b))


def combined(c, diagonals):
    x = cat([cat([diagonals[t, p] for p in range(2)], 0) for t in range(2)], 1)
    w = mm_rows(big_of(c), split(x))
    return cat([w[p * 128 : (p + 1) * 128, t * 256 : (t + 1) * 256] for p in range(2) for t in range(2)], 0)


def rows_gate(m, c):
    left, diagonals = lane_bit((64, 128), 64), {}
    for p in range(2):
        for t in range(2):
            x = rows_of(m, p * 2 + t, 64)
            y = pltpu.roll(x, 64, 1)
            blocks = [
                cat([jnp.where(left, up, 0.0), jnp.where(left, 0.0, down)], 0)
                for up, down in ((x, y), (y, x))
            ]
            diagonals[t, p] = cat(blocks, 1)
    return combined(c, diagonals)


def put(refs, x):
    refs[0][...], refs[1][...] = split(x)


def prepare(gr, gi, *rest):
    outs, (vr, vi, sems) = [rest[k : k + 2] for k in range(0, 20, 2)], rest[20:]
    l01, m0, c0, l25, w12, w3, w4, w56, l67, w7 = outs
    refs = (vr, vi)
    copies = []
    for s in range(8):
        at = pl.ds(s * 384, 384)
        copies.append(
            [pltpu.make_async_copy(a.at[at], b.at[at], sems.at[s, p]) for p, (a, b) in enumerate(((gr, vr), (gi, vi)))]
        )
        for copy in copies[s]:
            copy.start()

    def ready(s):
        for copy in copies[s]:
            copy.wait()

    sel, second = selector(0), selector(1)
    ready(0)
    put(m0, both(odd_even, refs, 1))
    put(c0, both(gate, refs, 2))
    ready(1)
    put(l01, turned(product(both(gate, refs, 3), both(gate, refs, 0))))
    ready(2)
    moved = columns_moved(
        cat([both(odd_even, refs, 4), both(odd_even, refs, 7), both(gate, refs, 6)], 0), sel
    )
    w1 = rows_gate(rows_of(moved, 0, 256), both(gate, refs, 5))
    w2 = rows_gate(rows_of(moved, 1, 256), both(odd_even, refs, 8))
    put(w12, product(w2, w1))
    ready(3)
    put(w3, rows_gate(columns_moved(both(odd_even, refs, 10), second), both(gate, refs, 11)))
    x = product(both(gate, refs, 9), rows_of(moved, 2, 256))
    ready(4)
    ready(5)
    y = product(both(odd_even, refs, 15), both(gate, refs, 12))
    put(l25, product(y, x))
    ready(6)
    ready(7)
    moved = columns_moved(
        cat([both(odd_even, refs, k) for k in (13, 16, 19, 22)] + [both(gate, refs, 18)], 0), sel
    )
    put(w4, rows_gate(rows_of(moved, 0, 256), both(gate, refs, 14)))
    w5 = rows_gate(rows_of(moved, 1, 256), both(gate, refs, 17))
    w6 = rows_gate(rows_of(moved, 2, 256), both(odd_even, refs, 20))
    put(w56, product(w6, w5))
    put(l67, turned(product(both(gate, refs, 21), rows_of(moved, 4, 256))))
    w = rows_gate(rows_of(moved, 3, 256), both(gate, refs, 23))
    put(w7, cat([columns_moved(w[:, :128], sel), columns_moved(w[:, 128:], sel)], 1))


def turned(x):
    n = x.shape[0] // 2
    return cat([x[:n].T, x[n:].T], 0)


def read_turned(h, l):
    return tuple(big(a[:128], -a[128:]) for a in (h[...], l[...]))


def read_big(h, l):
    return tuple(big(a[:128], a[128:]) for a in (h[...], l[...]))


def read_blocks(ref):
    return cat(
        [cat([ref[:, p, t].reshape(128, 128) for t in range(2)], 0) for p in range(2)], 1
    )


def read_strided(ref):
    return cat(
        [cat([ref[pl.ds(p * 4 + o, 64, 8), :] for o in range(4)], 0) for p in range(2)], 1
    )


def phase0(sr, si, out, vr, vi, vm, sems):
    fetches, sends = [], []
    for k in range(4):
        at = pl.ds(k * 4, 4)
        for p, (a, b) in enumerate(((sr, vr), (si, vi))):
            fetches.append(pltpu.make_async_copy(a.at[at], b.at[at], sems.at[p, k]))
            fetches[-1].start()
    for k in range(4):
        at = pl.ds(k * 4, 4)
        for p, b in enumerate((vr, vi)):
            fetches[2 * k + p].wait()
            vm[at, p] = b[at]
        sends.append(pltpu.make_async_copy(vm.at[at], out.at[at], sems.at[2, k]))
        sends[-1].start()
    for send in sends:
        send.wait()


def phase1(x, l01h, l01l, m0h, m0l, c0h, c0l, l25h, l25l, out):
    y = cat([x[:, p].reshape(256, 128) for p in range(2)], 1)
    y = mm_rows(split(y), read_turned(l01h, l01l))
    half = lambda a, k: a[:, k * 128 : (k + 1) * 128]
    y = cat([cat([rows_of(half(y, p), h, 128) for h in range(2)], 1) for p in range(2)], 0)
    y = mm_rows(read_big(m0h, m0l), split(y))
    rows = [cat([half(rows_of(y, 2 * p + t, 64), h) for t in range(2)], 1) for p in range(2) for h in range(2)]
    y = mm_rows(read_big(c0h, c0l), split(cat(rows, 0)))
    o = [rows_of(y, p, 128) for p in range(2)]
    o = [cat([half(a, 0), half(a, 1)], 0) for a in o]
    u = [swap(o[p][:128], o[p][128:], 1) for p in range(2)]
    rows = [u[p][v] for p in range(2) for v in range(2)]
    u = cat([cat([rows_of(r, f, 64) for r in rows], 0) for f in range(2)], 1)
    v = mm_rows(read_big(l25h, l25l), split(u))
    for p in range(2):
        for f in range(2):
            block = v[p * 128 : (p + 1) * 128, f * 128 : (f + 1) * 128]
            for t, y in enumerate(swap(block[:64], block[64:], 1)):
                out[pl.ds(p * 4 + t * 2 + f, 64, 8), :] = y


def phase2(x, w12h, w12l, w3h, w3l, out):
    o = applied(w12h, w12l, split(read_strided(x)))
    u = [swap(o[p][:128], o[p][128:], 1) for p in range(2)]
    rows = [u[p][v] for p in range(2) for v in range(2)]
    u = cat([cat([rows_of(r, a, 64) for a in range(2)], 1) for r in rows], 0)
    o = applied(w3h, w3l, split(u), NT)
    for p in range(2):
        for t in range(2):
            out[:, p, t] = rows_of(o[p], t, 128).reshape(16, 8, 128)


def phase3(x, w4h, w4l, w56h, w56l, l67h, l67l, out):
    o = applied(w4h, w4l, split(read_blocks(x)))
    rows = []
    for p in range(2):
        pairs = [swap(rows_of(o[p], 2 * t, 64), rows_of(o[p], 2 * t + 1, 64), 64) for t in range(2)]
        rows += [cat([pairs[0][v], pairs[1][v]], 1) for v in range(2)]
    o = applied(w56h, w56l, split(cat(rows, 0)), NT)
    z = mm_rows(split(cat(o, 1)), read_turned(l67h, l67l))
    for p in range(2):
        for k in range(4):
            out[pl.ds(p * 4 + k, 64, 8), :] = z[k * 64 : (k + 1) * 64, p * 128 : (p + 1) * 128]


def phase4(x, w7h, w7l, out_real, out_imag):
    o = applied(w7h, w7l, split(read_strided(x)))
    for ref, part in zip((out_real, out_imag), o):
        for t in range(2):
            ref[pl.ds(t, 128, 2), :] = rows_of(part, t, 128)


PARAMS = pltpu.CompilerParams(vmem_limit_bytes=48 << 20)
HILO512 = [jax.ShapeDtypeStruct((512, 256), BF16)] * 2
HILO256 = [jax.ShapeDtypeStruct((256, 128), BF16)] * 2


def call(kernel, name, out_shape, flops, *args, scratch=None, out_specs=None):
    more = {}
    if scratch is not None:
        in_hbm = pl.BlockSpec(memory_space=pltpu.HBM)
        more = {"in_specs": [in_hbm] * len(args), "scratch_shapes": scratch}
    if out_specs is not None:
        more["out_specs"] = out_specs
    return pl.pallas_call(
        kernel,
        out_shape=out_shape,
        compiler_params=PARAMS,
        cost_estimate=pl.CostEstimate(flops=flops, bytes_accessed=4 << 20, transcendentals=0),
        name=name,
        **more,
    )(*args)


def on_device(state_real, state_imag, gate_real, gate_imag):
    shape = state_real.shape
    sr, si, gr, gi = (
        pltpu.with_memory_space_constraint(a, pltpu.HBM)
        for a in (
            state_real.reshape(16, 16, 128), state_imag.reshape(16, 16, 128),
            gate_real.reshape(3072, 128), gate_imag.reshape(3072, 128),
        )
    )
    rows = jax.ShapeDtypeStruct((512, 128), F32)
    blocks = jax.ShapeDtypeStruct((16, 2, 2, 8, 128), F32)

    def far(x):
        return lax.all_to_all(x.reshape(16, 32, 128), "far", 0, 0, tiled=True)

    def near(x):
        x = lax.all_to_all(x.reshape(64, 8, 128), "near", 0, 0, tiled=True)
        return x.reshape(512, 128)

    x = call(
        phase0, "phase0", jax.ShapeDtypeStruct((16, 2, 16, 128), F32), 1 << 20, sr, si,
        scratch=[pltpu.VMEM((16, 16, 128), F32)] * 2
        + [pltpu.VMEM((16, 2, 16, 128), F32), pltpu.SemaphoreType.DMA((3, 4))],
        out_specs=pl.BlockSpec(memory_space=pltpu.HBM),
    )
    x = far(x)
    w = call(
        prepare, "prepare",
        HILO256 * 4 + HILO512 * 4 + HILO256 + HILO512, 2400 << 20,
        gr, gi, scratch=[pltpu.VMEM((3072, 128), F32)] * 2 + [pltpu.SemaphoreType.DMA((8, 2))],
    )
    x = near(call(phase1, "phase1", rows, 200 << 20, x.reshape(16, 2, 16, 128), *w[:8]))
    x = far(call(phase2, "phase2", blocks, 200 << 20, x, *w[8:12])).reshape(16, 2, 2, 8, 128)
    x = near(call(phase3, "phase3", rows, 200 << 20, x, *w[12:18]))
    flat = jax.ShapeDtypeStruct((256, 128), F32)
    real, imag = call(phase4, "phase4", [flat, flat], 200 << 20, x, *w[18:])
    return real.reshape(shape), imag.reshape(shape)


def solution(mesh):
    spec = P("far", "near", None, None, None)
    return jax.shard_map(
        on_device,
        mesh=mesh,
        in_specs=(spec, spec, P(), P()),
        out_specs=(spec, spec),
        check_vma=False,
    )
```

```python
import functools

import jax
import jax.numpy as jnp
from jax import lax
from jax.experimental import pallas as pl
from jax.experimental.pallas import tpu as pltpu
from jax.sharding import PartitionSpec as P

F32, BF16 = jnp.float32, jnp.bfloat16
NN = (((1,), (0,)), ((), ()))
NT = (((1,), (1,)), ((), ()))


def split(x):
    hi = x.astype(BF16)
    return hi, (x - hi.astype(F32)).astype(BF16)


def mm(a, b, dims=NN):
    dot = functools.partial(lax.dot_general, dimension_numbers=dims, preferred_element_type=F32)
    k = 0 if dims is NT else 1
    r = dot(a[0], cat(b, k))
    n = r.shape[1] // 2
    return r[:, :n] + (r[:, n:] + dot(a[1], b[0]))


def mm_rows(a, b, dims=NN, step=128):
    n = a[0].shape[0]
    return cat([mm(tuple(p[k : k + step] for p in a), b, dims) for k in range(0, n, step)], 0)


def cat(parts, axis):
    return jnp.concatenate(parts, axis)


def rows_of(x, n, count):
    return x[n * count : (n + 1) * count]


def merged(r, n):
    k = r.shape[1] // 2
    return r[:n, :k] - r[n:, k:], r[n:, :k] + r[:n, k:]


def applied(h, l, x, dims=NN):
    parts = []
    for k in range(0, 256, 128):
        w = tuple(cat([ref[pl.ds(k, 128), :], ref[pl.ds(256 + k, 128), :]], 0) for ref in (h, l))
        parts.append(merged(mm(w, x, dims), 128))
    return tuple(cat([p[k] for p in parts], 0) for k in range(2))


def big(real, imag):
    return cat([cat([real, -imag], 1), cat([imag, real], 1)], 0)


def lane_bit(shape, stride):
    return (lax.broadcasted_iota(jnp.int32, shape, 1) // stride) % 2 == 0


def swap(a, b, stride):
    even, lanes = lane_bit(a.shape, stride), a.shape[1]
    return (
        jnp.where(even, a, pltpu.roll(b, stride, 1)),
        jnp.where(even, pltpu.roll(a, lanes - stride, 1), b),
    )


def selector(bit):
    i = lax.broadcasted_iota(jnp.int32, (128, 128), 0)
    j = lax.broadcasted_iota(jnp.int32, (128, 128), 1)
    low, top = i % (1 << bit), i // 64
    mid = (i % 64) // (1 << bit)
    return jnp.where(j == mid * (2 << bit) + top * (1 << bit) + low, 1.0, 0.0).astype(BF16)


def columns_moved(x, sel):
    dot = functools.partial(lax.dot_general, dimension_numbers=NT, preferred_element_type=F32)
    hi, lo = split(x)
    return dot(hi, sel) + dot(lo, sel)


def gate(ref, at):
    return ref[pl.ds(at * 128, 128), :]


def odd_even(ref, at):
    return cat([ref[pl.ds(at * 128 + t, 64, 2), :] for t in range(2)], 0)


def both(read, refs, at):
    return cat([read(ref, at) for ref in refs], 0)


def big_of(x):
    n = x.shape[0] // 2
    return tuple(big(a[:n], a[n:]) for a in split(x))


def product(a, b):
    return mm_rows(big_of(a), split(b))


def combined(c, diagonals):
    x = cat([cat([diagonals[t, p] for p in range(2)], 0) for t in range(2)], 1)
    w = mm_rows(big_of(c), split(x))
    return cat([w[p * 128 : (p + 1) * 128, t * 256 : (t + 1) * 256] for p in range(2) for t in range(2)], 0)


def rows_gate(m, c):
    left, diagonals = lane_bit((64, 128), 64), {}
    for p in range(2):
        for t in range(2):
            x = rows_of(m, p * 2 + t, 64)
            y = pltpu.roll(x, 64, 1)
            blocks = [
                cat([jnp.where(left, up, 0.0), jnp.where(left, 0.0, down)], 0)
                for up, down in ((x, y), (y, x))
            ]
            diagonals[t, p] = cat(blocks, 1)
    return combined(c, diagonals)


def put(refs, x):
    refs[0][...], refs[1][...] = split(x)


def prepare(gr, gi, *rest):
    outs, (vr, vi, sems) = [rest[k : k + 2] for k in range(0, 20, 2)], rest[20:]
    l01, m0, c0, l25, w12, w3, w4, w56, l67, w7 = outs
    refs = (vr, vi)
    copies = []
    for s in range(8):
        at = pl.ds(s * 384, 384)
        copies.append(
            [pltpu.make_async_copy(a.at[at], b.at[at], sems.at[s, p]) for p, (a, b) in enumerate(((gr, vr), (gi, vi)))]
        )
        for copy in copies[s]:
            copy.start()

    def ready(s):
        for copy in copies[s]:
            copy.wait()

    sel, second = selector(0), selector(1)
    ready(0)
    put(m0, both(odd_even, refs, 1))
    put(c0, both(gate, refs, 2))
    ready(1)
    put(l01, turned(product(both(gate, refs, 3), both(gate, refs, 0))))
    ready(2)
    moved = columns_moved(
        cat([both(odd_even, refs, 4), both(odd_even, refs, 7), both(gate, refs, 6)], 0), sel
    )
    w1 = rows_gate(rows_of(moved, 0, 256), both(gate, refs, 5))
    w2 = rows_gate(rows_of(moved, 1, 256), both(odd_even, refs, 8))
    put(w12, product(w2, w1))
    ready(3)
    put(w3, rows_gate(columns_moved(both(odd_even, refs, 10), second), both(gate, refs, 11)))
    x = product(both(gate, refs, 9), rows_of(moved, 2, 256))
    ready(4)
    ready(5)
    y = product(both(odd_even, refs, 15), both(gate, refs, 12))
    put(l25, product(y, x))
    ready(6)
    ready(7)
    moved = columns_moved(
        cat([both(odd_even, refs, k) for k in (13, 16, 19, 22)] + [both(gate, refs, 18)], 0), sel
    )
    put(w4, rows_gate(rows_of(moved, 0, 256), both(gate, refs, 14)))
    w5 = rows_gate(rows_of(moved, 1, 256), both(gate, refs, 17))
    w6 = rows_gate(rows_of(moved, 2, 256), both(odd_even, refs, 20))
    put(w56, product(w6, w5))
    put(l67, turned(product(both(gate, refs, 21), rows_of(moved, 4, 256))))
    w = rows_gate(rows_of(moved, 3, 256), both(gate, refs, 23))
    put(w7, cat([columns_moved(w[:, :128], sel), columns_moved(w[:, 128:], sel)], 1))


def turned(x):
    n = x.shape[0] // 2
    return cat([x[:n].T, x[n:].T], 0)


def read_turned(h, l):
    return tuple(big(a[:128], -a[128:]) for a in (h[...], l[...]))


def read_big(h, l):
    return tuple(big(a[:128], a[128:]) for a in (h[...], l[...]))


def read_blocks(ref):
    return cat(
        [cat([ref[:, p, t].reshape(128, 128) for t in range(2)], 0) for p in range(2)], 1
    )


def read_strided(ref):
    return cat(
        [cat([ref[pl.ds(p * 4 + o, 64, 8), :] for o in range(4)], 0) for p in range(2)], 1
    )


def phase0(sr, si, out, vr, vi, sems):
    pairs = [(sr, vr), (si, vi)]
    copies = [pltpu.make_async_copy(a, b, sems.at[p]) for p, (a, b) in enumerate(pairs)]
    for copy in copies:
        copy.start()
    for p, copy in enumerate(copies):
        copy.wait()
        out[:, p] = pairs[p][1][...]


def phase1(x, l01h, l01l, m0h, m0l, c0h, c0l, l25h, l25l, out):
    y = cat([x[:, p].reshape(256, 128) for p in range(2)], 1)
    y = mm_rows(split(y), read_turned(l01h, l01l))
    half = lambda a, k: a[:, k * 128 : (k + 1) * 128]
    y = cat([cat([rows_of(half(y, p), h, 128) for h in range(2)], 1) for p in range(2)], 0)
    y = mm_rows(read_big(m0h, m0l), split(y))
    rows = [cat([half(rows_of(y, 2 * p + t, 64), h) for t in range(2)], 1) for p in range(2) for h in range(2)]
    y = mm_rows(read_big(c0h, c0l), split(cat(rows, 0)))
    o = [rows_of(y, p, 128) for p in range(2)]
    o = [cat([half(a, 0), half(a, 1)], 0) for a in o]
    u = [swap(o[p][:128], o[p][128:], 1) for p in range(2)]
    rows = [u[p][v] for p in range(2) for v in range(2)]
    u = cat([cat([rows_of(r, f, 64) for r in rows], 0) for f in range(2)], 1)
    v = mm_rows(read_big(l25h, l25l), split(u))
    for p in range(2):
        for f in range(2):
            block = v[p * 128 : (p + 1) * 128, f * 128 : (f + 1) * 128]
            for t, y in enumerate(swap(block[:64], block[64:], 1)):
                out[pl.ds(p * 4 + t * 2 + f, 64, 8), :] = y


def phase2(x, w12h, w12l, w3h, w3l, out):
    o = applied(w12h, w12l, split(read_strided(x)))
    u = [swap(o[p][:128], o[p][128:], 1) for p in range(2)]
    rows = [u[p][v] for p in range(2) for v in range(2)]
    u = cat([cat([rows_of(r, a, 64) for a in range(2)], 1) for r in rows], 0)
    o = applied(w3h, w3l, split(u), NT)
    for p in range(2):
        for t in range(2):
            out[:, p, t] = rows_of(o[p], t, 128).reshape(16, 8, 128)


def phase3(x, w4h, w4l, w56h, w56l, l67h, l67l, out):
    o = applied(w4h, w4l, split(read_blocks(x)))
    rows = []
    for p in range(2):
        pairs = [swap(rows_of(o[p], 2 * t, 64), rows_of(o[p], 2 * t + 1, 64), 64) for t in range(2)]
        rows += [cat([pairs[0][v], pairs[1][v]], 1) for v in range(2)]
    o = applied(w56h, w56l, split(cat(rows, 0)), NT)
    z = mm_rows(split(cat(o, 1)), read_turned(l67h, l67l))
    for p in range(2):
        for k in range(4):
            out[pl.ds(p * 4 + k, 64, 8), :] = z[k * 64 : (k + 1) * 64, p * 128 : (p + 1) * 128]


def phase4(x, w7h, w7l, out_real, out_imag):
    o = applied(w7h, w7l, split(read_strided(x)))
    for ref, part in zip((out_real, out_imag), o):
        for t in range(2):
            ref[pl.ds(t, 128, 2), :] = rows_of(part, t, 128)


PARAMS = pltpu.CompilerParams(vmem_limit_bytes=48 << 20)
HILO512 = [jax.ShapeDtypeStruct((512, 256), BF16)] * 2
HILO256 = [jax.ShapeDtypeStruct((256, 128), BF16)] * 2


def call(kernel, name, out_shape, flops, *args, scratch=None, out_specs=None):
    more = {}
    if scratch is not None:
        in_hbm = pl.BlockSpec(memory_space=pltpu.HBM)
        more = {"in_specs": [in_hbm] * len(args), "scratch_shapes": scratch}
    if out_specs is not None:
        more["out_specs"] = out_specs
    return pl.pallas_call(
        kernel,
        out_shape=out_shape,
        compiler_params=PARAMS,
        cost_estimate=pl.CostEstimate(flops=flops, bytes_accessed=4 << 20, transcendentals=0),
        name=name,
        **more,
    )(*args)


def on_device(state_real, state_imag, gate_real, gate_imag):
    shape = state_real.shape
    sr, si, gr, gi = (
        pltpu.with_memory_space_constraint(a, pltpu.HBM)
        for a in (
            state_real.reshape(16, 16, 128), state_imag.reshape(16, 16, 128),
            gate_real.reshape(3072, 128), gate_imag.reshape(3072, 128),
        )
    )
    rows = jax.ShapeDtypeStruct((512, 128), F32)
    blocks = jax.ShapeDtypeStruct((16, 2, 2, 8, 128), F32)

    def far(x):
        return lax.all_to_all(x.reshape(16, 32, 128), "far", 0, 0, tiled=True)

    def near(x):
        x = lax.all_to_all(x.reshape(64, 8, 128), "near", 0, 0, tiled=True)
        return x.reshape(512, 128)

    x = call(
        phase0, "phase0", jax.ShapeDtypeStruct((16, 2, 16, 128), F32), 1 << 20, sr, si,
        scratch=[pltpu.VMEM((16, 16, 128), F32)] * 2 + [pltpu.SemaphoreType.DMA((2,))],
    )
    x = far(x)
    w = call(
        prepare, "prepare",
        HILO256 * 4 + HILO512 * 4 + HILO256 + HILO512, 2400 << 20,
        gr, gi, scratch=[pltpu.VMEM((3072, 128), F32)] * 2 + [pltpu.SemaphoreType.DMA((8, 2))],
    )
    x = near(call(phase1, "phase1", rows, 200 << 20, x.reshape(16, 2, 16, 128), *w[:8]))
    x = far(call(phase2, "phase2", blocks, 200 << 20, x, *w[8:12])).reshape(16, 2, 2, 8, 128)
    x = near(call(phase3, "phase3", rows, 200 << 20, x, *w[12:18]))
    flat = jax.ShapeDtypeStruct((256, 128), F32)
    real, imag = call(phase4, "phase4", [flat, flat], 200 << 20, x, *w[18:])
    return real.reshape(shape), imag.reshape(shape)


def solution(mesh):
    spec = P("far", "near", None, None, None)
    return jax.shard_map(
        on_device,
        mesh=mesh,
        in_specs=(spec, spec, P(), P()),
        out_specs=(spec, spec),
        check_vma=False,
    )
```
